128 devices in a mesh: dp: 16 (over x, y), tensor: 8 (over z, core).
Axes of the slice: x: 4, y: 4, z: 4, core: 2. Of those that a mesh axis runs over, the one named last changes fastest.
Arguments:
- hidden_in: bfloat16 [6144, 4096], P('dp', 'tensor'), may hold values from -48 to 48
- encodings: bfloat16 [1024, 128, 896], P('dp', 'tensor'), may hold values from -48 to 48
- nbr_shard: int32 [96, 2], P('dp'), may hold values from 0 to 15, all different within a row; in each aligned block of 6 rows (0 to 5, 6 to 11, ...) at most 2 rows name the same one
- nbr_row: int32 [96, 2], P('dp'), may hold values from 0 to 63
- w_query: bfloat16 [4096, 4096], P(None, 'tensor'), may hold values from -0.09375 to 0.09375
- w_key: bfloat16 [896, 4096], P(None, 'tensor'), may hold values from -0.1875 to 0.1875
- w_value: bfloat16 [896, 4096], P(None, 'tensor'), may hold values from -0.1875 to 0.1875
- w_output: bfloat16 [4096, 4096], P('tensor'), may hold values from -0.09375 to 0.09375
- cotangent: bfloat16 [6144, 4096], P('dp', 'tensor'), may hold values from -6 to 6
Outputs:
- layer_out: bfloat16 [6144, 4096], P('dp', 'tensor')
- grad_hidden: bfloat16 [6144, 4096], P('dp', 'tensor')
- grad_encodings: float32 [1024, 128, 896], P('dp', 'tensor')
- grad_query: float32 [4096, 4096], P('dp', 'tensor')
- grad_key: float32 [896, 4096], P('dp', 'tensor')
- grad_value: float32 [896, 4096], P('dp', 'tensor')
- grad_output: float32 [4096, 4096], P('tensor', 'dp')
The draws below stay inside these ranges and needn't reach their ends.
Inputs may be any that keep to these rules, and one draw needn't show every extreme that they name: `nbr_shard`: in the 6 spans of one index of dp no shard is named more than 2 times, and one is named exactly 2 times in some of them; the 2 shards of a span differ.
All inputs are finite; a program needn't handle non-finite values.
Results may differ from the reference program's by a relative error of at most 0.02.
Values may be sent and summed in bfloat16 or wider, within the bound.
A program may use at most 128 MiB of HBM per device.

```python
import math
import jax
import jax.numpy as jnp
import numpy as np
from jax import lax

D = 4096
HEADS = 32
HD = 128
E = 896
SPAN = 64
NB = 128
K_NBR = 2
TOK_DEV = 384
DB_DEV = 64
TOKENS = 6144
SPAN_DEV = 6
SPANS = 96
LIVE = 12
CAP = 2
DB_ROWS = 1024
COLS_TP = 512
N_DP = 16
N_TENSOR = 8


def spread_normal(key, shape):
    first = jax.random.fold_in(key, 0)
    base = jax.random.normal(first, shape, jnp.float32)
    return jnp.clip(base, -6.0, 6.0)


def draw_hidden_in(key, part):
    return spread_normal(jax.random.fold_in(key, 11), (TOKENS, D)).astype(jnp.bfloat16)


def draw_encodings(key, part):
    return spread_normal(jax.random.fold_in(key, 23), (DB_ROWS, NB, E)).astype(jnp.bfloat16)


def plant(values, own_key, least, high):
    longest = values.shape.index(max(values.shape))
    spots = []
    for shift in (0, 1):
        where = [jax.random.randint(jax.random.fold_in(own_key, axis), (), 0, length) for axis, length in enumerate(values.shape)]
        where[longest] = (where[longest] + shift) % values.shape[longest]
        spots.append(tuple(where))
    return values.at[spots[0]].set(least).at[spots[1]].set(high)


def shard_levels(stream_key, shape, cuts, least, high):
    gain = 1.0
    for dim, blocks in cuts:
        draws = jax.random.uniform(jax.random.fold_in(jax.random.fold_in(stream_key, 6), dim), (blocks,), jnp.float32, least / len(cuts), high / len(cuts))
        gain = gain * jnp.repeat(jnp.exp(draws), shape[dim] // blocks).reshape((-1,) + (1,) * (len(shape) - 1 - dim))
    return gain


def deal_out(own_key, own, number, rows, number_of, top, limit, slope):
    order = jax.random.permutation(own_key, number_of)
    packed, ordinary = shares(number_of, rows * top, limit, slope, True), shares(number_of, rows * top, limit, slope, False)
    places = jnp.arange(number_of)

    def named(sizes, rotation):
        used = int((sizes > 0).sum())
        fixed = max(1, used // 4)
        passed = fixed + (places - fixed + rotation * (used - fixed)) % max(1, number_of - fixed)
        return jnp.zeros((number_of,), jnp.int32).at[order[jnp.where(places < fixed, places, passed)]].set(jnp.asarray(sizes, jnp.int32))

    sizes = jnp.where(number % 4 == 0, named(packed, number // 4), named(ordinary, number - number // 4 - 1))
    mixed = jax.random.permutation(jax.random.fold_in(own, 3), number_of)
    giver, taker = mixed[0:number_of // 2 * 2:2], mixed[1:number_of // 2 * 2:2]
    margin = jnp.minimum(sizes[giver] - 1, limit - sizes[taker]) // 2
    margin = jnp.where((giver == order[0]) | (taker == order[0]) | (sizes[taker] == 0), 0, jnp.maximum(margin, 0))
    passed = jax.random.randint(jax.random.fold_in(own, 4), (number_of // 2,), 0, 1 << 20) % (margin + 1)
    sizes = sizes.at[giver].add(-passed).at[taker].add(passed)
    labels = jnp.searchsorted(jnp.cumsum(sizes), jnp.arange(rows * top), side="right").astype(jnp.int32)
    table = labels.reshape(top, rows).T
    table = table[jax.random.permutation(jax.random.fold_in(own, 1), rows)]
    rotation = jax.random.randint(jax.random.fold_in(own, 2), (rows, 1), 0, top)
    return jnp.take_along_axis(table, (jnp.arange(top)[None, :] + rotation) % top, axis=1)


def shares(count, total, bound, slope, full):
    weights = [(1 << 20) // math.isqrt(rank ** slope) + 1 for rank in range(1, count + 1)]
    largest = bound if full else min(bound, max(-(-total // count), total * weights[0] // sum(weights)))
    least = 1 if total - largest >= count - 1 else 0
    holding, surplus = [largest] + [least] * (count - 1), total - largest - least * (count - 1)
    while surplus > 0:
        candidates = [i for i in range(1, count) if holding[i] < largest] or [i for i in range(1, count) if holding[i] < bound]
        pool, remaining = sum([weights[i] for i in candidates]), surplus
        for i in candidates:
            addition = min(bound - holding[i], max(1, remaining * weights[i] // pool), surplus)
            holding[i] = holding[i] + addition
            surplus = surplus - addition
    return np.array(holding)


def centred(key, shape, scale, bound, shards=(), kind=jnp.bfloat16):
    entries = jax.random.normal(key, shape, jnp.float32) * scale
    if len(shards) > 0:
        entries = shard_levels(key, shape, shards, -0.22, 0.18) * entries
    return jnp.clip(entries, min=-bound, max=bound).astype(kind)


def setup_inputs(seed: int = 0) -> dict:
    key_list = jax.random.split(jax.random.key(seed), 10)
    hidden_in = draw_hidden_in(jax.random.fold_in(key_list[9], 71), 0)
    encodings = draw_encodings(jax.random.fold_in(key_list[9], 71), 0)
    nbr_shard_keys = jax.random.split(jax.random.fold_in(key_list[2], 1), SPANS // SPAN_DEV)
    nbr_shard_turns = jax.random.permutation(jax.random.fold_in(key_list[2], 3), SPANS // SPAN_DEV)
    nbr_shard = jax.vmap(lambda own, number: deal_out(jax.random.fold_in(key_list[2], 2), own, number, SPAN_DEV, N_DP, K_NBR, CAP, 2))(nbr_shard_keys, nbr_shard_turns).reshape((SPANS, K_NBR))
    nbr_row = plant(jax.random.randint(key_list[3], (SPANS, K_NBR), 0, DB_DEV), jax.random.fold_in(key_list[3], 1), 0, DB_DEV - 1).astype(jnp.int32)
    w_query = centred(key_list[4], (D, D), D ** -0.5, 0.09375, ((1, 8),))
    w_key = centred(key_list[5], (E, D), E ** -0.5, 0.1875, ((1, 8),))
    w_value = centred(key_list[6], (E, D), E ** -0.5, 0.1875, ((1, 8),))
    w_output = centred(key_list[7], (D, D), D ** -0.5, 0.09375, ((0, 8),))
    cotangent = centred(key_list[8], (TOKENS, D), 1.0, 6.0, ((0, 16), (1, 8)))
    return {"hidden_in": hidden_in, "encodings": encodings, "nbr_shard": nbr_shard, "nbr_row": nbr_row, "w_query": w_query, "w_key": w_key, "w_value": w_value, "w_output": w_output, "cotangent": cotangent}


def rounded(value):
    return lax.optimization_barrier(value.astype(jnp.bfloat16)).astype(jnp.float32)

def block_products(left, right, rows):
    left_blocks = left.reshape(-1, rows, left.shape[1])
    right_blocks = right.reshape(-1, rows, right.shape[1])

    def step(total, pair):
        part = jnp.dot(pair[0].T, pair[1], preferred_element_type=jnp.float32)
        return (total + rounded(part), None)
    start = jnp.zeros((left.shape[1], right.shape[1]), jnp.float32)
    total, unused = lax.scan(step, start, (left_blocks, right_blocks))
    return total

def reference(hidden_in, encodings, nbr_shard, nbr_row, w_query, w_key, w_value, w_output, cotangent):
    scale = 1.0 / math.sqrt(HD)
    query = jnp.dot(hidden_in, w_query, preferred_element_type=jnp.float32).astype(jnp.bfloat16)
    ids = (nbr_shard * DB_DEV + nbr_row).reshape(-1).astype(jnp.int32)
    flat_nbr = encodings[ids].reshape(-1, E)
    keys = jnp.dot(flat_nbr, w_key, preferred_element_type=jnp.float32).astype(jnp.bfloat16)
    values = jnp.dot(flat_nbr, w_value, preferred_element_type=jnp.float32).astype(jnp.bfloat16)
    qh = query.reshape(SPANS, SPAN, HEADS, HD).astype(jnp.float32)
    kh = keys.reshape(SPANS, K_NBR * NB, HEADS, HD).astype(jnp.float32)
    vh = values.reshape(SPANS, K_NBR * NB, HEADS, HD).astype(jnp.float32)
    scores = jnp.einsum('cqhd,ckhd->chqk', qh, kh) * scale
    probs = jax.nn.softmax(scores, axis=-1)
    probs_b = probs.astype(jnp.bfloat16).astype(jnp.float32)
    attended = jnp.einsum('chqk,ckhd->cqhd', probs_b, vh).astype(jnp.bfloat16).reshape(TOKENS, D)
    layer_out = jnp.dot(attended, w_output, preferred_element_type=jnp.float32).astype(jnp.bfloat16)
    grad_att = jnp.dot(cotangent, w_output.T, preferred_element_type=jnp.float32).astype(jnp.bfloat16)
    dah = grad_att.reshape(SPANS, SPAN, HEADS, HD).astype(jnp.float32)
    grad_prob = jnp.einsum('cqhd,ckhd->chqk', dah, vh)
    inner = lax.optimization_barrier(jnp.sum(grad_prob * probs, axis=-1, keepdims=True))
    grad_score = (probs * (grad_prob - inner) * scale).astype(jnp.bfloat16).astype(jnp.float32)
    grad_v = jnp.einsum('chqk,cqhd->ckhd', probs_b, dah).astype(jnp.bfloat16).reshape(-1, D)
    grad_q = jnp.einsum('chqk,ckhd->cqhd', grad_score, kh).astype(jnp.bfloat16).reshape(TOKENS, D)
    grad_k = jnp.einsum('chqk,cqhd->ckhd', grad_score, qh).astype(jnp.bfloat16).reshape(-1, D)
    grad_hidden = jnp.dot(grad_q, w_query.T, preferred_element_type=jnp.float32).astype(jnp.bfloat16)
    grad_nbr = jnp.zeros((grad_k.shape[0], E), jnp.float32)
    for part in range(N_TENSOR):
        low = part * COLS_TP
        high = low + COLS_TP
        term = jnp.dot(grad_k[:, low:high], w_key[:, low:high].T, preferred_element_type=jnp.float32)
        term = term + jnp.dot(grad_v[:, low:high], w_value[:, low:high].T, preferred_element_type=jnp.float32)
        grad_nbr = grad_nbr + rounded(term)
    grad_encodings = jnp.zeros((DB_ROWS, NB, E), jnp.float32).at[ids].add(grad_nbr.reshape(-1, NB, E))
    grad_query = block_products(hidden_in, grad_q, TOK_DEV)
    grad_key = block_products(flat_nbr, grad_k, LIVE * NB)
    grad_value = block_products(flat_nbr, grad_v, LIVE * NB)
    grad_output = block_products(attended, cotangent, TOK_DEV)
    return (layer_out, grad_hidden, grad_encodings, grad_query, grad_key, grad_value, grad_output)
```

```python
import math

import jax
import jax.numpy as jnp
from jax import lax
from jax.experimental import pallas as pl
from jax.experimental.pallas import tpu as pltpu
from jax.sharding import PartitionSpec as P

HD = 128
SPAN = 64
NB = 128
K_NBR = 2
MESH = pl.DeviceIdType.MESH
BF = jnp.bfloat16
F32 = jnp.float32
ANY = pl.BlockSpec(memory_space=pl.ANY)
VM = pl.BlockSpec(memory_space=pltpu.VMEM)
SM = pl.BlockSpec(memory_space=pltpu.SMEM)
DMA = pltpu.SemaphoreType.DMA
NT = (((1,), (1,)), ((), ()))
TN = (((0,), (0,)), ((), ()))


def mm(a, b):
    return jnp.dot(a, b, preferred_element_type=F32)


def mm_nt(a, b):
    return lax.dot_general(a, b, NT, preferred_element_type=F32)


def mm_tn(a, b):
    return lax.dot_general(a, b, TN, preferred_element_type=F32)


class Place:
    def __init__(self):
        self.d = lax.axis_index("dp")
        self.t = lax.axis_index("tensor")
        self.x, self.y = self.d // 4, self.d % 4
        self.z, self.c = self.t // 2, self.t % 2
        self.partner = self.z * 2 + (1 - self.c)
        self.tr = ((self.z + 1) % 4) * 2 + self.c
        self.tl = ((self.z + 3) % 4) * 2 + self.c
        self.tf = ((self.z + 2) % 4) * 2 + self.c

    def peer(self, n):
        return (self.d + n) % 16

    def source(self, n):
        return (self.d + 16 - n) % 16

    def greet(self):
        barrier = pltpu.get_barrier_semaphore()
        for other in (self.partner, self.tr, self.tl):
            pl.semaphore_signal(barrier, inc=1, device_id=(self.d, other), device_id_type=MESH)

        @pl.loop(1, 16)
        def _(n):
            pl.semaphore_signal(barrier, inc=1, device_id=(self.peer(n), self.t), device_id_type=MESH)

        pl.semaphore_wait(barrier, 18)


def remote(src, dst, send, recv, dev):
    return pltpu.make_async_remote_copy(
        src_ref=src, dst_ref=dst, send_sem=send, recv_sem=recv, device_id=dev, device_id_type=MESH
    )


class Gather:
    def __init__(self, me, buf, half, send, recv):
        self.me, self.buf, self.half, self.send, self.recv = me, buf, half, send, recv

    def copy(self, n, t, dev, part=None):
        view = self.buf.at[t] if part is None else self.buf.at[t, pl.ds(part * self.half, self.half)]
        return remote(view, view, self.send.at[n], self.recv.at[n], (self.me.d, dev))

    def start(self):
        me = self.me
        self.copy(0, me.t, me.tr).start()
        self.copy(1, me.t, me.tl).start()
        self.copy(4, me.t, me.partner).start()

    def forward(self):
        me = self.me
        self.copy(0, me.tl, me.tr).wait_recv()
        self.copy(2, me.tl, me.tr, 0).start()
        self.copy(5, me.tl, me.partner).start()
        self.copy(1, me.tr, me.tl).wait_recv()
        self.copy(3, me.tr, me.tl, 1).start()
        self.copy(6, me.tr, me.partner).start()

    def far(self):
        me = self.me
        self.copy(2, me.tf, me.tr, 0).wait_recv()
        self.copy(3, me.tf, me.tl, 1).wait_recv()
        self.copy(7, me.tf, me.partner).start()

    def other(self, t):
        return t + 1 - 2 * self.me.c

    def pairs(self):
        me = self.me
        for n, t in ((4, me.t), (5, me.tl), (6, me.tr), (7, me.tf)):
            self.copy(n, self.other(t), me.partner).wait_recv()

    def sent(self):
        me = self.me
        self.copy(0, me.t, me.tr).wait_send()
        self.copy(1, me.t, me.tl).wait_send()
        self.copy(2, me.tl, me.tr, 0).wait_send()
        self.copy(3, me.tr, me.tl, 1).wait_send()
        for n, t in ((4, me.t), (5, me.tl), (6, me.tr), (7, me.tf)):
            self.copy(n, t, me.partner).wait_send()


def gather_kernel(
    shard_s, row_s, hid, cot, enc, wq, wo, wk, wv,
    q_o, ga_o, k_o, v_o, h_o, c_o, n_o, want_o,
    H, C, N, encv, outg, arr, req, wanted, want_s, wqv, wov, wkv, wvv, acc,
    load, zs, zr, rs, rr, fs, fr,
):
    me = Place()
    d, t = me.d, me.t
    loads = [
        pltpu.make_async_copy(hid, H.at[t], load.at[0]),
        pltpu.make_async_copy(cot, C.at[t], load.at[1]),
        pltpu.make_async_copy(enc, encv, load.at[2]),
        pltpu.make_async_copy(wq, wqv, load.at[3]),
        pltpu.make_async_copy(wo, wov, load.at[4]),
        pltpu.make_async_copy(wk, wkv, load.at[5]),
        pltpu.make_async_copy(wv, wvv, load.at[6]),
    ]
    for one in loads:
        one.start()
    owners, slots = [], []
    lane = lax.broadcasted_iota(jnp.int32, (8, 128), 1)
    table = jnp.full((8, 128), 0, jnp.int32)
    for k in range(12):
        owner = shard_s[k // 2, k % 2]
        position = jnp.int32(0)
        for other in owners:
            position = position + (other == owner).astype(jnp.int32)
        owners.append(owner)
        slots.append((owner, jnp.minimum(position, 1)))
        table = jnp.where(lane == owner * 2 + position, row_s[k // 2, k % 2], table)
    req[...] = table
    wanted[d] = table
    me.greet()

    def request(n, dst):
        return remote(req, wanted.at[dst], rs.at[n], rr.at[n], (me.peer(n), t))

    @pl.loop(1, 16)
    def _(n):
        request(n, d).start()

    gh = Gather(me, H, 192, zs.at[0], zr.at[0])
    gc = Gather(me, C, 192, zs.at[1], zr.at[1])
    gn = Gather(me, N, 96, zs.at[2], zr.at[2])
    loads[0].wait()
    gh.start()
    loads[1].wait()
    gc.start()
    loads[2].wait()

    @pl.loop(1, 16)
    def _(n):
        request(n, me.source(n)).wait_recv()

    to_s = pltpu.make_async_copy(wanted, want_s, load.at[7])
    to_s.start()
    to_s.wait()

    def fetch(n, dst):
        return remote(outg.at[me.peer(n)], arr.at[dst], fs.at[n], fr.at[n], (me.peer(n), t))

    @pl.loop(1, 16)
    def _(n):
        reader = me.peer(n)
        for p in range(2):
            outg[reader, p] = encv[want_s[reader, 0, d * 2 + p]]
        fetch(n, d).start()

    for p in range(2):
        arr[d, p] = encv[want_s[d, 0, d * 2 + p]]
    gh.forward()

    @pl.loop(1, 16)
    def _(n):
        fetch(n, me.source(n)).wait_recv()

    for k in range(12):
        owner, position = slots[k]
        N[t, k * 16:(k + 1) * 16, :] = arr[owner, position]
    gn.start()
    gc.forward()
    gh.far()
    loads[3].wait()
    gh.pairs()
    h_out = pltpu.make_async_copy(H, h_o, load.at[8])
    h_out.start()
    want_o[...] = wanted[...]
    acc[...] = jnp.zeros_like(acc)

    @pl.loop(0, 8)
    def _(k):
        acc[...] += mm(H[k], wqv[k])

    q_o[...] = acc[...].astype(BF)
    gn.forward()
    gc.far()
    loads[4].wait()
    gc.pairs()
    c_out = pltpu.make_async_copy(C, c_o, load.at[9])
    c_out.start()
    acc[...] = jnp.zeros_like(acc)

    @pl.loop(0, 8)
    def _(k):
        acc[...] += mm_nt(C[k], wov[:, pl.ds(pl.multiple_of(k * 512, 512), 512)])

    ga_o[...] = acc[...].astype(BF)
    gn.far()
    loads[5].wait()
    loads[6].wait()
    gn.pairs()
    n_out = pltpu.make_async_copy(N, n_o, load.at[10])
    n_out.start()

    @pl.loop(0, 8)
    def _(k):
        k_o[k] = mm(N[k], wkv[...]).astype(BF)
        v_o[k] = mm(N[k], wvv[...]).astype(BF)

    gh.sent()
    gc.sent()
    gn.sent()

    @pl.loop(1, 16)
    def _(n):
        request(n, d).wait_send()
        fetch(n, d).wait_send()

    h_out.wait()
    c_out.wait()
    n_out.wait()


def gather_call(nbr_shard, nbr_row, hidden_in, cotangent, encodings, wq, wo, wk, wv):
    S = jax.ShapeDtypeStruct
    return pl.pallas_call(
        gather_kernel,
        name="gather",
        out_shape=(
            S((384, 512), BF), S((384, 512), BF), S((8, 192, 512), BF), S((8, 192, 512), BF),
            S((8, 384, 512), BF), S((8, 384, 512), BF), S((8, 192, 896), BF), S((16, 8, 128), jnp.int32),
        ),
        in_specs=[SM, SM] + [ANY] * 7,
        out_specs=(VM, VM, VM, VM, ANY, ANY, ANY, VM),
        scratch_shapes=[
            pltpu.VMEM((8, 384, 512), BF),
            pltpu.VMEM((8, 384, 512), BF),
            pltpu.VMEM((8, 192, 896), BF),
            pltpu.VMEM((64, 16, 896), BF),
            pltpu.VMEM((16, 2, 16, 896), BF),
            pltpu.VMEM((16, 2, 16, 896), BF),
            pltpu.VMEM((8, 128), jnp.int32),
            pltpu.VMEM((16, 8, 128), jnp.int32),
            pltpu.SMEM((16, 8, 128), jnp.int32),
            pltpu.VMEM((8, 512, 512), BF),
            pltpu.VMEM((512, 4096), BF),
            pltpu.VMEM((896, 512), BF),
            pltpu.VMEM((896, 512), BF),
            pltpu.VMEM((384, 512), F32),
            DMA((11,)), DMA((3, 8)), DMA((3, 8)), DMA((16,)), DMA((16,)), DMA((16,)), DMA((16,)),
        ],
        compiler_params=pltpu.CompilerParams(
            collective_id=1, has_side_effects=True, vmem_limit_bytes=56 * 2**20
        ),
    )(nbr_shard, nbr_row, hidden_in, cotangent, encodings, wq, wo, wk, wv)


def attend_kernel(q_ref, ga_ref, k_ref, v_ref, att_ref, gq_ref, gk_ref, gv_ref):
    scale = 1.0 / math.sqrt(HD)
    for h in range(4):
        cols = slice(h * HD, (h + 1) * HD)
        q, ga = q_ref[:, cols], ga_ref[:, cols]
        k = k_ref[:, :, cols].reshape(256, HD)
        v = v_ref[:, :, cols].reshape(256, HD)
        s = mm_nt(q, k) * scale
        e = jnp.exp(s - jnp.max(s, axis=-1, keepdims=True))
        p = e / jnp.sum(e, axis=-1, keepdims=True)
        pb = p.astype(BF)
        att_ref[:, cols] = mm(pb, v).astype(BF)
        gp = mm_nt(ga, v)
        inner = jnp.sum(gp * p, axis=-1, keepdims=True)
        gs = (p * (gp - inner) * scale).astype(BF)
        gv_ref[:, :, cols] = mm_tn(pb, ga).astype(BF).reshape(8, 32, HD)
        gq_ref[:, cols] = mm(gs, k).astype(BF)
        gk_ref[:, :, cols] = mm_tn(gs, q).astype(BF).reshape(8, 32, HD)


def attend_call(q, ga, k, v):
    S = jax.ShapeDtypeStruct
    tok = pl.BlockSpec((SPAN, 512), lambda i: (i, 0))
    nbr = pl.BlockSpec((8, 32, 512), lambda i: (0, i, 0))
    return pl.pallas_call(
        attend_kernel,
        name="attend",
        grid=(6,),
        out_shape=(S((384, 512), BF), S((384, 512), BF), S((8, 192, 512), BF), S((8, 192, 512), BF)),
        in_specs=[tok, tok, nbr, nbr],
        out_specs=(tok, tok, nbr, nbr),
        compiler_params=pltpu.CompilerParams(vmem_limit_bytes=32 * 2**20),
    )(q, ga, k, v)


class Ring:
    def __init__(self, group, f1, f2, send, recv, pos, right, left):
        self.group, self.f1, self.f2 = group, f1, f2
        self.pos = pos
        self.r1, self.r2, self.l1 = (pos + 1) % 4, (pos + 2) % 4, (pos + 3) % 4

        def cp(n, src, dst, dev):
            return remote(src, dst, send.at[n], recv.at[n], dev)

        self.s = [
            cp(0, group(self.r2, 0), f1.at[0], right),
            cp(1, group(self.r2, 1), f1.at[1], left),
            cp(2, group(self.r1, 1), f2.at[0, 1], right),
            cp(3, group(self.l1, 0), f2.at[1, 0], left),
            cp(4, group(self.r1, 0), f2.at[0, 0], right),
            cp(5, group(self.l1, 1), f2.at[1, 1], left),
        ]

    def first(self):
        self.s[0].start()
        self.s[1].start()

    def second(self):
        self.s[2].start()
        self.s[3].start()

    def middle(self):
        self.s[0].wait_recv()
        add_into(self.group(self.r1, 0), self.f1.at[0])
        self.s[4].start()
        self.s[1].wait_recv()
        add_into(self.group(self.l1, 1), self.f1.at[1])
        self.s[5].start()

    def arrive(self):
        for n in range(2, 6):
            self.s[n].wait_recv()

    def sum_in_place(self):
        for h in range(2):
            add_into(self.group(self.pos, h), self.f2.at[0, h], self.f2.at[1, h])

    def total(self, h):
        return (
            self.group(self.pos, h)[...].astype(F32)
            + self.f2[0, h].astype(F32)
            + self.f2[1, h].astype(F32)
        )

    def sent(self):
        for n in range(6):
            self.s[n].wait_send()


def add_into(dst, *srcs):
    lead, rows = dst.shape[:-2], dst.shape[-2]
    step = 32 if rows % 32 == 0 else 16

    def part(*where):
        value = dst[where].astype(F32)
        for src in srcs:
            value = value + src[where].astype(F32)
        dst[where] = value.astype(BF)

    if lead:

        @pl.loop(0, lead[0])
        def _(q):
            @pl.loop(0, rows // step)
            def _(r):
                part(q, pl.ds(pl.multiple_of(r * step, step), step))
    else:

        @pl.loop(0, rows // step)
        def _(r):
            part(pl.ds(pl.multiple_of(r * step, step), step))


def reduce_kernel(
    shard_s, att, gq, gk, gv, h_i, c_i, n_i, wq, wo, wk, wv,
    out_o, hid_o, ret_o, gq_o, gk_o, gv_o, go_o,
    attv, gqv, attT, gqT, gkv, gvv, H, C, N, W, wkv, wvv, GK, GV,
    Bq, Bo, Ba, Bb, q1, q2, o1, o2, a1, a2, b1, b2, q3, q4, o3, o4, a3, a4, b3, b4,
    T, Uo, Po, Uh, Ph, Tn, Un, Pn, zo1, zo2, zh1, zh2, zn1, zn2, live, spread, ret,
    load, wload, ps, pr, ss, sr, fs, fr,
):
    me = Place()
    d, t, c = me.d, me.t, me.c
    loads = [
        pltpu.make_async_copy(src, dst, load.at[n])
        for n, (src, dst) in enumerate(
            (
                (att, attv), (gq, gqv), (h_i, H), (c_i, C), (gk, gkv), (gv, gvv),
                (wk, wkv), (wv, wvv), (n_i, N),
            )
        )
    ]
    for one in loads:
        one.start()

    right_x = ((me.x + 1) % 4 * 4 + me.y, t)
    left_x = ((me.x + 3) % 4 * 4 + me.y, t)
    right_y = (me.x * 4 + (me.y + 1) % 4, t)
    left_y = (me.x * 4 + (me.y + 3) % 4, t)
    right_z, left_z = (d, me.tr), (d, me.tl)
    along = {"x": (me.x, right_x, left_x), "y": (me.y, right_y, left_y), "z": (me.z, right_z, left_z)}

    def ring(n, group, f1, f2, axis):
        return Ring(group, f1, f2, ss.at[n], sr.at[n], *along[axis])

    def pair(n, buf, f1, f2, f3, f4, first, second):
        mine = along[first][0]
        one = ring(n, lambda g, h: buf.at[g, h], f1, f2, first)
        two = ring(n + 1, lambda g, h: buf.at[mine, g // 2, (g % 2) * 2 + h], f3, f4, second)
        return one, two

    rq, rq2 = pair(0, Bq, q1, q2, q3, q4, "x", "y")
    ro, ro2 = pair(2, Bo, o1, o2, o3, o4, "y", "x")
    ra, ra2 = pair(4, Ba, a1, a2, a3, a4, "x", "y")
    rb, rb2 = pair(6, Bb, b1, b2, b3, b4, "y", "x")
    zo = ring(8, lambda g, h: Uo.at[g, h], zo1, zo2, "z")
    zh = ring(9, lambda g, h: Uh.at[g, h], zh1, zh2, "z")
    zn = ring(10, lambda g, h: Un.at[g, h], zn1, zn2, "z")

    loads[0].wait()
    loads[1].wait()
    attT[...] = attv[...].T
    gqT[...] = gqv[...].T
    live[12] = jnp.zeros((16, 896), BF)
    loads[2].wait()
    loads[3].wait()
    me.greet()

    def weights(group_x, group_y):
        @pl.loop(0, 4)
        def _(s):
            dq = group_x * 4 + s
            do = s * 4 + group_y
            value = mm(gqT[...], H[dq // 2, :, pl.ds(pl.multiple_of((dq % 2) * 256, 256), 256)]).astype(BF)
            Bq[group_x, s // 2, (s % 2) * 2] = value[:256]
            Bq[group_x, s // 2, (s % 2) * 2 + 1] = value[256:]
            value = mm(attT[...], C[do // 2, :, pl.ds(pl.multiple_of((do % 2) * 256, 256), 256)]).astype(BF)
            Bo[group_y, s // 2, (s % 2) * 2] = value[:256]
            Bo[group_y, s // 2, (s % 2) * 2 + 1] = value[256:]

    weights(rq.r2, ro.r2)
    rq.first()
    ro.first()

    def nbr_terms(core, dst):
        @pl.loop(0, 4)
        def _(zz):
            tt = zz * 2 + core
            value = (mm_nt(gkv[tt], wkv[...]) + mm_nt(gvv[tt], wvv[...])).astype(BF)
            dst[zz, 0] = value[:96]
            dst[zz, 1] = value[96:]

    def streamed(left, core, dst, product):
        @pl.loop(0, 4)
        def _(zz):
            value = product(left, zz * 2 + core).astype(BF)
            dst[zz, 0] = value[:192]
            dst[zz, 1] = value[192:]

    def share(n, T, P):
        return remote(T, P, ps.at[n], pr.at[n], (d, me.partner))

    sn, so, sh = share(0, Tn, Pn), share(1, T, Po), share(2, T, Ph)
    for n in range(4, 8):
        loads[n].wait()
    nbr_terms(1 - c, Tn)
    sn.start()
    weights(rq.r1, ro.r1)
    weights(rq.l1, ro.l1)
    rq.second()
    ro.second()
    nbr_terms(c, Un)

    def out_product(left, tt):
        return mm(left[...], W[tt])

    def hid_product(left, tt):
        return mm_nt(left[...], W[tt])

    w_load = [pltpu.make_async_copy(wo.at[:, pl.ds(n * 512, 512)], W.at[n], wload.at[n]) for n in range(8)]
    w_load.append(pltpu.make_async_copy(wq, W, wload.at[8]))
    for n in range(8):
        w_load[n].start()
    sn.wait_recv()

    def merge(U, P):
        @pl.loop(0, 4)
        def _(zz):
            for h in range(2):
                add_into(U.at[zz, h], P.at[zz, h])

    merge(Un, Pn)
    zn.first()
    zn.second()
    for n in range(8):
        w_load[n].wait()
    streamed(attv, 1 - c, T, out_product)
    so.start()
    streamed(attv, c, Uo, out_product)
    w_load[8].start()
    so.wait_recv()
    merge(Uo, Po)
    zo.first()
    zo.second()
    zn.middle()
    rq.middle()
    ro.middle()
    w_load[8].wait()
    so.wait_send()
    streamed(gqv, 1 - c, T, hid_product)
    sh.start()
    streamed(gqv, c, Uh, hid_product)
    sh.wait_recv()
    merge(Uh, Ph)
    zh.first()
    zh.second()
    weights(rq.pos, ro.pos)
    loads[8].wait()

    @pl.loop(0, 7)
    def _(m):
        cols = pl.ds(pl.multiple_of(m * 128, 128), 128)
        left = N[:, :, cols].reshape(1536, 128)
        GK[cols, :] = mm_tn(left, gkv[...].reshape(1536, 512))
        GV[cols, :] = mm_tn(left, gvv[...].reshape(1536, 512))

    @pl.loop(0, 16)
    def _(dd):
        rows = pl.ds(pl.multiple_of(dd * 56, 8), 56)
        value = jnp.concatenate([GK[rows, :], GV[rows, :]], axis=0).astype(BF)
        xx, yy = dd // 4, dd % 4
        Ba[xx, yy // 2, (yy % 2) * 2] = value[:, :128]
        Ba[xx, yy // 2, (yy % 2) * 2 + 1] = value[:, 128:256]
        Bb[yy, xx // 2, (xx % 2) * 2] = value[:, 256:384]
        Bb[yy, xx // 2, (xx % 2) * 2 + 1] = value[:, 384:]

    ra.first()
    rb.first()
    ra.second()
    rb.second()
    zn.arrive()
    for h in range(2):
        value = zn.total(h).astype(BF)
        for k in range(6):
            live[h * 6 + k] = value[k * 16:(k + 1) * 16]
    owners, slots = [], []
    for k in range(12):
        owner = shard_s[k // 2, k % 2]
        position = jnp.int32(0)
        for other in owners:
            position = position + (other == owner).astype(jnp.int32)
        owners.append(owner)
        slots.append(owner * 2 + position)

    def give(n, dst):
        return remote(spread.at[me.peer(n)], ret.at[dst], fs.at[n], fr.at[n], (me.peer(n), t))

    def choose(o, p):
        where = jnp.int32(12)
        for k in range(12):
            where = jnp.where(slots[k] == o * 2 + p, jnp.int32(k), where)
        return where

    @pl.loop(1, 16)
    def _(n):
        o = me.peer(n)
        for p in range(2):
            spread[o, p] = live[choose(o, p)]
        give(n, d).start()

    for p in range(2):
        ret[d, p] = live[choose(d, p)]
    zo.middle()
    zh.middle()
    rq.arrive()
    rq.sum_in_place()
    rq2.first()
    rq2.second()
    ro.arrive()
    ro.sum_in_place()
    ro2.first()
    ro2.second()
    ra.middle()
    rb.middle()
    zo.arrive()
    for h in range(2):
        out_o[h * 192:(h + 1) * 192, :] = zo.total(h).astype(BF)
    zh.arrive()
    for h in range(2):
        hid_o[h * 192:(h + 1) * 192, :] = zh.total(h).astype(BF)
    rq2.middle()
    ro2.middle()
    ra.arrive()
    ra.sum_in_place()
    ra2.first()
    ra2.second()
    rb.arrive()
    rb.sum_in_place()
    rb2.first()
    rb2.second()
    rq2.arrive()
    for h in range(2):
        gq_o[:, h * 256:(h + 1) * 256] = rq2.total(h).T
    ro2.arrive()
    for h in range(2):
        go_o[h * 256:(h + 1) * 256, :] = ro2.total(h)
    ra2.middle()
    rb2.middle()

    @pl.loop(1, 16)
    def _(n):
        give(n, me.source(n)).wait_recv()

    ret_o[...] = ret[...]
    ra2.arrive()
    rb2.arrive()
    for h in range(2):
        for base, one in ((0, ra2), (256, rb2)):
            value = one.total(h)
            low = base + h * 128
            gk_o[:, low:low + 128] = value[:56]
            gv_o[:, low:low + 128] = value[56:]
    for one in (rq, ro, ra, rb, rq2, ro2, ra2, rb2, zo, zh, zn):
        one.sent()
    for one in (sn, sh):
        one.wait_send()

    @pl.loop(1, 16)
    def _(n):
        give(n, d).wait_send()


def reduce_call(nbr_shard, att, gq, gk, gv, h, cc, n, wq, wo, wk, wv):
    S = jax.ShapeDtypeStruct
    V = pltpu.VMEM
    big = [V((4, 2, 4, 256, 256), BF)] * 2 + [V((4, 2, 4, 112, 128), BF)] * 2
    first = []
    for r, w in ((256, 256), (256, 256), (112, 128), (112, 128)):
        first += [V((2, 4, r, w), BF), V((2, 2, 4, r, w), BF)]
    second = []
    for r, w in ((256, 256), (256, 256), (112, 128), (112, 128)):
        second += [V((2, r, w), BF), V((2, 2, r, w), BF)]
    terms = [V((4, 2, 192, 512), BF)] * 5 + [V((4, 2, 96, 896), BF)] * 3
    rings = []
    for r, w in ((192, 512), (192, 512), (96, 896)):
        rings += [V((2, r, w), BF), V((2, 2, r, w), BF)]
    return pl.pallas_call(
        reduce_kernel,
        name="reduce",
        out_shape=(
            S((384, 512), BF), S((384, 512), BF), S((16, 2, 16, 896), BF),
            S((256, 512), F32), S((56, 512), F32), S((56, 512), F32), S((512, 256), F32),
        ),
        in_specs=[SM] + [ANY] * 11,
        out_specs=(VM,) * 7,
        scratch_shapes=[
            V((384, 512), BF), V((384, 512), BF), V((512, 384), BF), V((512, 384), BF),
            V((8, 192, 512), BF), V((8, 192, 512), BF), V((8, 384, 512), BF), V((8, 384, 512), BF),
            V((8, 192, 896), BF), V((8, 512, 512), BF), V((896, 512), BF), V((896, 512), BF),
            V((896, 512), F32), V((896, 512), F32),
        ]
        + big + first + second + terms + rings
        + [
            V((13, 16, 896), BF), V((16, 2, 16, 896), BF), V((16, 2, 16, 896), BF),
            DMA((9,)), DMA((9,)), DMA((3,)), DMA((3,)), DMA((11, 6)), DMA((11, 6)), DMA((16,)), DMA((16,)),
        ],
        compiler_params=pltpu.CompilerParams(
            collective_id=2, has_side_effects=True, vmem_limit_bytes=64 * 2**20 - 2**17
        ),
    )(nbr_shard, att, gq, gk, gv, h, cc, n, wq, wo, wk, wv)


def scatter_kernel(want_s, ret_ref, out_ref):
    out_ref[...] = jnp.zeros_like(out_ref)

    @pl.loop(0, 32)
    def _(s):
        row = want_s[s]
        out_ref[row] += ret_ref[s].astype(F32)


def scatter_call(want, ret):
    return pl.pallas_call(
        scatter_kernel,
        name="scatter",
        out_shape=jax.ShapeDtypeStruct((64, 16, 896), F32),
        in_specs=[SM, VM],
        out_specs=VM,
        compiler_params=pltpu.CompilerParams(vmem_limit_bytes=32 * 2**20),
    )(want, ret)


def shards(hidden_in, encodings, nbr_shard, nbr_row, w_query, w_key, w_value, w_output, cotangent):
    wq = w_query.reshape(8, 512, 512)
    q, ga, k, v, h, c, n, wanted = gather_call(
        nbr_shard, nbr_row, hidden_in, cotangent, encodings, wq, w_output, w_key, w_value
    )
    att, gq, gk, gv = attend_call(q, ga, k, v)
    out, hid, ret, sq, sk, sv, so = reduce_call(
        nbr_shard, att, gq, gk, gv, h, c, n, wq, w_output, w_key, w_value
    )
    d = lax.axis_index("dp")
    want = lax.dynamic_slice(wanted[:, 0, :], (0, d * 2), (16, 2)).reshape(32)
    enc = scatter_call(want, ret.reshape(32, 16, 896))
    return (out, hid, enc, sq, sk, sv, so)


def solution(mesh):
    return jax.shard_map(
        shards,
        mesh=mesh,
        in_specs=(
            P("dp", "tensor"),
            P("dp", "tensor", None),
            P("dp", None),
            P("dp", None),
            P(None, "tensor"),
            P(None, "tensor"),
            P(None, "tensor"),
            P("tensor", None),
            P("dp", "tensor"),
        ),
        out_specs=(
            P("dp", "tensor"),
            P("dp", "tensor"),
            P("dp", "tensor", None),
            P("dp", "tensor"),
            P("dp", "tensor"),
            P("dp", "tensor"),
            P("tensor", "dp"),
        ),
        check_vma=False,
    )
```

```python
import math

import jax
import jax.numpy as jnp
from jax import lax
from jax.experimental import pallas as pl
from jax.experimental.pallas import tpu as pltpu
from jax.sharding import PartitionSpec as P

HD = 128
SPAN = 64
NB = 128
K_NBR = 2
MESH = pl.DeviceIdType.MESH
BF = jnp.bfloat16
F32 = jnp.float32
ANY = pl.BlockSpec(memory_space=pl.ANY)
VM = pl.BlockSpec(memory_space=pltpu.VMEM)
SM = pl.BlockSpec(memory_space=pltpu.SMEM)
DMA = pltpu.SemaphoreType.DMA
NT = (((1,), (1,)), ((), ()))
TN = (((0,), (0,)), ((), ()))


def mm(a, b):
    return jnp.dot(a, b, preferred_element_type=F32)


def mm_nt(a, b):
    return lax.dot_general(a, b, NT, preferred_element_type=F32)


def mm_tn(a, b):
    return lax.dot_general(a, b, TN, preferred_element_type=F32)


class Place:
    def __init__(self):
        self.d = lax.axis_index("dp")
        self.t = lax.axis_index("tensor")
        self.x, self.y = self.d // 4, self.d % 4
        self.z, self.c = self.t // 2, self.t % 2
        self.partner = self.z * 2 + (1 - self.c)
        self.tr = ((self.z + 1) % 4) * 2 + self.c
        self.tl = ((self.z + 3) % 4) * 2 + self.c
        self.tf = ((self.z + 2) % 4) * 2 + self.c

    def peer(self, n):
        return (self.d + n) % 16

    def source(self, n):
        return (self.d + 16 - n) % 16

    def greet(self):
        barrier = pltpu.get_barrier_semaphore()
        for other in (self.partner, self.tr, self.tl):
            pl.semaphore_signal(barrier, inc=1, device_id=(self.d, other), device_id_type=MESH)

        @pl.loop(1, 16)
        def _(n):
            pl.semaphore_signal(barrier, inc=1, device_id=(self.peer(n), self.t), device_id_type=MESH)

        pl.semaphore_wait(barrier, 18)


def remote(src, dst, send, recv, dev):
    return pltpu.make_async_remote_copy(
        src_ref=src, dst_ref=dst, send_sem=send, recv_sem=recv, device_id=dev, device_id_type=MESH
    )


class Gather:
    def __init__(self, me, buf, half, send, recv):
        self.me, self.buf, self.half, self.send, self.recv = me, buf, half, send, recv

    def copy(self, n, t, dev, part=None):
        view = self.buf.at[t] if part is None else self.buf.at[t, pl.ds(part * self.half, self.half)]
        return remote(view, view, self.send.at[n], self.recv.at[n], (self.me.d, dev))

    def start(self):
        me = self.me
        self.copy(0, me.t, me.tr).start()
        self.copy(1, me.t, me.tl).start()
        self.copy(4, me.t, me.partner).start()

    def forward(self):
        me = self.me
        self.copy(0, me.tl, me.tr).wait_recv()
        self.copy(2, me.tl, me.tr, 0).start()
        self.copy(5, me.tl, me.partner).start()
        self.copy(1, me.tr, me.tl).wait_recv()
        self.copy(3, me.tr, me.tl, 1).start()
        self.copy(6, me.tr, me.partner).start()

    def far(self):
        me = self.me
        self.copy(2, me.tf, me.tr, 0).wait_recv()
        self.copy(3, me.tf, me.tl, 1).wait_recv()
        self.copy(7, me.tf, me.partner).start()

    def other(self, t):
        return t + 1 - 2 * self.me.c

    def near_pairs(self):
        me = self.me
        for n, t in ((4, me.t), (5, me.tl), (6, me.tr)):
            self.copy(n, self.other(t), me.partner).wait_recv()

    def last_pair(self):
        self.copy(7, self.other(self.me.tf), self.me.partner).wait_recv()

    def pairs(self):
        self.near_pairs()
        self.last_pair()

    def sent(self):
        me = self.me
        self.copy(0, me.t, me.tr).wait_send()
        self.copy(1, me.t, me.tl).wait_send()
        self.copy(2, me.tl, me.tr, 0).wait_send()
        self.copy(3, me.tr, me.tl, 1).wait_send()
        for n, t in ((4, me.t), (5, me.tl), (6, me.tr), (7, me.tf)):
            self.copy(n, t, me.partner).wait_send()


def attend(q_ref, ga_ref, k_ref, v_ref, att_ref, gq_ref, gk_ref, gv_ref, rows, keys):
    scale = 1.0 / math.sqrt(HD)
    heads = [slice(h * HD, (h + 1) * HD) for h in range(4)]
    q, ga = [q_ref[rows, c] for c in heads], [ga_ref[rows, c] for c in heads]
    k = [k_ref[:, keys, c].reshape(256, HD) for c in heads]
    v = [v_ref[:, keys, c].reshape(256, HD) for c in heads]
    s = [mm_nt(a, b) * scale for a, b in zip(q, k)]
    gp = [mm_nt(a, b) for a, b in zip(ga, v)]
    e = [jnp.exp(a - jnp.max(a, axis=-1, keepdims=True)) for a in s]
    p = [a * (1.0 / jnp.sum(a, axis=-1, keepdims=True)) for a in e]
    pb = [a.astype(BF) for a in p]
    inner = [jnp.sum(a * b, axis=-1, keepdims=True) for a, b in zip(gp, p)]
    gs = [(a * (b - c) * scale).astype(BF) for a, b, c in zip(p, gp, inner)]
    for n, c in enumerate(heads):
        att_ref[rows, c] = mm(pb[n], v[n]).astype(BF)
        gq_ref[rows, c] = mm(gs[n], k[n]).astype(BF)
    for n, c in enumerate(heads):
        gv_ref[:, keys, c] = mm_tn(pb[n], ga[n]).astype(BF).reshape(8, 32, HD)
        gk_ref[:, keys, c] = mm_tn(gs[n], q[n]).astype(BF).reshape(8, 32, HD)


def gather_kernel(
    shard_s, row_s, hid, cot, enc, wq, wo, wk, wv,
    att_o, gq_o, gk_o, gv_o, h_o, c_o, n_o, want_o,
    qv, gav, kv, vv, H, C, N, encv, outg, arr, req, wanted, want_s, wqv, wov, wkv, wvv,
    load, zs, zr, rs, rr, fs, fr,
):
    me = Place()
    d, t = me.d, me.t
    loads = [
        pltpu.make_async_copy(hid, H.at[t], load.at[0]),
        pltpu.make_async_copy(cot, C.at[t], load.at[1]),
        pltpu.make_async_copy(enc, encv, load.at[2]),
        pltpu.make_async_copy(wq, wqv, load.at[3]),
        pltpu.make_async_copy(wo, wov, load.at[4]),
        pltpu.make_async_copy(wk, wkv, load.at[5]),
        pltpu.make_async_copy(wv, wvv, load.at[6]),
    ]
    for one in loads:
        one.start()
    owners, slots = [], []
    lane = lax.broadcasted_iota(jnp.int32, (8, 128), 1)
    table = jnp.full((8, 128), 0, jnp.int32)
    for k in range(12):
        owner = shard_s[k % 2, k // 2]
        position = jnp.int32(0)
        for other in owners:
            position = position + (other == owner).astype(jnp.int32)
        owners.append(owner)
        slots.append((owner, jnp.minimum(position, 1)))
        table = jnp.where(lane == owner * 2 + position, row_s[k % 2, k // 2], table)
    req[...] = table
    wanted[d] = table
    me.greet()

    def request(n, dst):
        return remote(req, wanted.at[dst], rs.at[n], rr.at[n], (me.peer(n), t))

    @pl.loop(1, 16)
    def _(n):
        request(n, d).start()

    gh = Gather(me, H, 192, zs.at[0], zr.at[0])
    gc = Gather(me, C, 192, zs.at[1], zr.at[1])
    gn = Gather(me, N, 96, zs.at[2], zr.at[2])
    loads[0].wait()
    gh.start()
    loads[1].wait()
    gc.start()
    loads[2].wait()

    @pl.loop(1, 16)
    def _(n):
        request(n, me.source(n)).wait_recv()

    to_s = pltpu.make_async_copy(wanted, want_s, load.at[7])
    to_s.start()
    to_s.wait()

    def fetch(n, dst):
        return remote(outg.at[me.peer(n)], arr.at[dst], fs.at[n], fr.at[n], (me.peer(n), t))

    @pl.loop(1, 16)
    def _(n):
        reader = me.peer(n)
        for p in range(2):
            outg[reader, p] = encv[want_s[reader, 0, d * 2 + p]]
        fetch(n, d).start()

    for p in range(2):
        arr[d, p] = encv[want_s[d, 0, d * 2 + p]]
    gh.forward()

    @pl.loop(1, 16)
    def _(n):
        fetch(n, me.source(n)).wait_recv()

    for k in range(12):
        owner, position = slots[k]
        N[t, k * 16:(k + 1) * 16, :] = arr[owner, position]
    gn.start()
    gc.forward()
    gh.far()
    for r in range(16):
        for p in range(2):
            want_o[r * 2 + p] = want_s[r, 0, d * 2 + p]
    loads[3].wait()
    gh.pairs()
    h_out = pltpu.make_async_copy(H, h_o, load.at[8])
    h_out.start()

    @pl.loop(0, 2)
    def _(m):
        cols = pl.ds(pl.multiple_of(m * 256, 256), 256)
        value = mm(H[0], wqv[0, :, cols])
        for k in range(1, 8):
            value = value + mm(H[k], wqv[k, :, cols])
        qv[:, cols] = value.astype(BF)

    gn.forward()
    loads[4].wait()
    loads[5].wait()
    loads[6].wait()

    def project(k):
        kv[k] = mm(N[k], wkv[...]).astype(BF)
        vv[k] = mm(N[k], wvv[...]).astype(BF)

    @pl.loop(0, 3)
    def _(s):
        project((me.z + (s + 3)) % 4 * 2 + me.c)

    gc.far()
    gn.near_pairs()

    @pl.loop(0, 3)
    def _(s):
        project((me.z + (s + 3)) % 4 * 2 + 1 - me.c)

    gc.pairs()
    c_out = pltpu.make_async_copy(C, c_o, load.at[9])
    c_out.start()
    gn.far()

    @pl.loop(0, 2)
    def _(m):
        cols = pl.ds(pl.multiple_of(m * 256, 256), 256)
        value = mm_nt(C[0], wov[cols, 0:512])
        for k in range(1, 8):
            value = value + mm_nt(C[k], wov[cols, k * 512:(k + 1) * 512])
        gav[:, cols] = value.astype(BF)

    project(me.tf)
    gn.last_pair()
    n_out = pltpu.make_async_copy(N, n_o, load.at[10])
    n_out.start()
    project((me.z + 2) % 4 * 2 + 1 - me.c)

    @pl.loop(0, 6, unroll=2)
    def _(s):
        rows = pl.ds(pl.multiple_of(s * 64, 64), 64)
        keys = pl.ds(pl.multiple_of(s * 32, 32), 32)
        attend(qv, gav, kv, vv, att_o, gq_o, gk_o, gv_o, rows, keys)

    gh.sent()
    gc.sent()
    gn.sent()

    @pl.loop(1, 16)
    def _(n):
        request(n, d).wait_send()
        fetch(n, d).wait_send()

    h_out.wait()
    c_out.wait()
    n_out.wait()


def gather_call(nbr_shard, nbr_row, hidden_in, cotangent, encodings, wq, wo, wk, wv):
    S = jax.ShapeDtypeStruct
    return pl.pallas_call(
        gather_kernel,
        name="gather",
        out_shape=(
            S((384, 512), BF), S((384, 512), BF), S((8, 192, 512), BF), S((8, 192, 512), BF),
            S((8, 384, 512), BF), S((8, 384, 512), BF), S((8, 192, 896), BF), S((32,), jnp.int32),
        ),
        in_specs=[SM, SM] + [ANY] * 7,
        out_specs=(VM, VM, VM, VM, ANY, ANY, ANY, SM),
        scratch_shapes=[
            pltpu.VMEM((384, 512), BF),
            pltpu.VMEM((384, 512), BF),
            pltpu.VMEM((8, 192, 512), BF),
            pltpu.VMEM((8, 192, 512), BF),
            pltpu.VMEM((8, 384, 512), BF),
            pltpu.VMEM((8, 384, 512), BF),
            pltpu.VMEM((8, 192, 896), BF),
            pltpu.VMEM((64, 16, 896), BF),
            pltpu.VMEM((16, 2, 16, 896), BF),
            pltpu.VMEM((16, 2, 16, 896), BF),
            pltpu.VMEM((8, 128), jnp.int32),
            pltpu.VMEM((16, 8, 128), jnp.int32),
            pltpu.SMEM((16, 8, 128), jnp.int32),
            pltpu.VMEM((8, 512, 512), BF),
            pltpu.VMEM((512, 4096), BF),
            pltpu.VMEM((896, 512), BF),
            pltpu.VMEM((896, 512), BF),
            DMA((11,)), DMA((3, 8)), DMA((3, 8)), DMA((16,)), DMA((16,)), DMA((16,)), DMA((16,)),
        ],
        compiler_params=pltpu.CompilerParams(
            collective_id=1, has_side_effects=True, vmem_limit_bytes=56 * 2**20
        ),
    )(nbr_shard, nbr_row, hidden_in, cotangent, encodings, wq, wo, wk, wv)


class Ring:
    def __init__(self, group, f1, f2, send, recv, pos, right, left):
        self.group, self.f1, self.f2 = group, f1, f2
        self.pos = pos
        self.r1, self.r2, self.l1 = (pos + 1) % 4, (pos + 2) % 4, (pos + 3) % 4

        def cp(n, src, dst, dev):
            return remote(src, dst, send.at[n], recv.at[n], dev)

        self.s = [
            cp(0, group(self.r2, 0), f1.at[0], right),
            cp(1, group(self.r2, 1), f1.at[1], left),
            cp(2, group(self.r1, 1), f2.at[0, 1], right),
            cp(3, group(self.l1, 0), f2.at[1, 0], left),
            cp(4, group(self.r1, 0), f2.at[0, 0], right),
            cp(5, group(self.l1, 1), f2.at[1, 1], left),
        ]

    def first(self):
        self.s[0].start()
        self.s[1].start()

    def second(self):
        self.s[2].start()
        self.s[3].start()

    def middle(self):
        self.s[0].wait_recv()
        add_into(self.group(self.r1, 0), self.f1.at[0])
        self.s[4].start()
        self.s[1].wait_recv()
        add_into(self.group(self.l1, 1), self.f1.at[1])
        self.s[5].start()

    def arrive(self):
        for n in range(2, 6):
            self.s[n].wait_recv()

    def sum_in_place(self):
        for h in range(2):
            add_into(self.group(self.pos, h), self.f2.at[0, h], self.f2.at[1, h])

    def total(self, h):
        return (
            self.group(self.pos, h)[...].astype(F32)
            + self.f2[0, h].astype(F32)
            + self.f2[1, h].astype(F32)
        )

    def sent(self):
        for n in range(6):
            self.s[n].wait_send()


def add_into(dst, *srcs):
    lead, rows = dst.shape[:-2], dst.shape[-2]
    step = 32 if rows % 32 == 0 else 16

    def part(*where):
        value = dst[where].astype(F32)
        for src in srcs:
            value = value + src[where].astype(F32)
        dst[where] = value.astype(BF)

    if lead:

        @pl.loop(0, lead[0])
        def _(q):
            @pl.loop(0, rows // step)
            def _(r):
                part(q, pl.ds(pl.multiple_of(r * step, step), step))
    else:

        @pl.loop(0, rows // step)
        def _(r):
            part(pl.ds(pl.multiple_of(r * step, step), step))


def reduce_kernel(
    shard_s, att, gq, gk, gv, h_i, c_i, n_i, wq, wo, wk, wv,
    out_o, hid_o, ret_o, gq_o, gk_o, gv_o, go_o,
    attv, gqv, attT, gqT, gkv, gvv, H, C, N, W, wkv, wvv, GK, GV,
    Bq, Bo, Ba, Bb, q1, q2, o1, o2, a1, a2, b1, b2, q3, q4, o3, o4, a3, a4, b3, b4,
    T, Uo, Po, Uh, Ph, Tn, Un, Pn, zo1, zo2, zh1, zh2, zn1, zn2, live, spread, ret,
    load, wload, ps, pr, ss, sr, fs, fr,
):
    me = Place()
    d, t, c = me.d, me.t, me.c
    loads = [
        pltpu.make_async_copy(src, dst, load.at[n])
        for n, (src, dst) in enumerate(
            (
                (att, attv), (gq, gqv), (h_i, H), (c_i, C), (gk, gkv), (gv, gvv),
                (wk, wkv), (wv, wvv), (n_i, N),
            )
        )
    ]
    for one in loads:
        one.start()

    right_x = ((me.x + 1) % 4 * 4 + me.y, t)
    left_x = ((me.x + 3) % 4 * 4 + me.y, t)
    right_y = (me.x * 4 + (me.y + 1) % 4, t)
    left_y = (me.x * 4 + (me.y + 3) % 4, t)
    right_z, left_z = (d, me.tr), (d, me.tl)
    along = {"x": (me.x, right_x, left_x), "y": (me.y, right_y, left_y), "z": (me.z, right_z, left_z)}

    def ring(n, group, f1, f2, axis):
        return Ring(group, f1, f2, ss.at[n], sr.at[n], *along[axis])

    def pair(n, buf, f1, f2, f3, f4, first, second):
        mine = along[first][0]
        one = ring(n, lambda g, h: buf.at[g, h], f1, f2, first)
        two = ring(n + 1, lambda g, h: buf.at[mine, g // 2, (g % 2) * 2 + h], f3, f4, second)
        return one, two

    rq, rq2 = pair(0, Bq, q1, q2, q3, q4, "x", "y")
    ro, ro2 = pair(2, Bo, o1, o2, o3, o4, "y", "x")
    ra, ra2 = pair(4, Ba, a1, a2, a3, a4, "x", "y")
    rb, rb2 = pair(6, Bb, b1, b2, b3, b4, "y", "x")
    zo = ring(8, lambda g, h: Uo.at[g, h], zo1, zo2, "z")
    zh = ring(9, lambda g, h: Uh.at[g, h], zh1, zh2, "z")
    zn = ring(10, lambda g, h: Un.at[g, h], zn1, zn2, "z")

    loads[0].wait()
    loads[1].wait()
    attT[...] = attv[...].T
    gqT[...] = gqv[...].T
    live[12] = jnp.zeros((16, 896), BF)
    loads[2].wait()
    loads[3].wait()
    me.greet()

    def weights(group_x, group_y):
        @pl.loop(0, 4)
        def _(s):
            dq = group_x * 4 + s
            do = s * 4 + group_y
            value = mm(gqT[...], H[dq // 2, :, pl.ds(pl.multiple_of((dq % 2) * 256, 256), 256)]).astype(BF)
            Bq[group_x, s // 2, (s % 2) * 2] = value[:256]
            Bq[group_x, s // 2, (s % 2) * 2 + 1] = value[256:]
            value = mm(attT[...], C[do // 2, :, pl.ds(pl.multiple_of((do % 2) * 256, 256), 256)]).astype(BF)
            Bo[group_y, s // 2, (s % 2) * 2] = value[:256]
            Bo[group_y, s // 2, (s % 2) * 2 + 1] = value[256:]

    weights(rq.r2, ro.r2)
    rq.first()
    ro.first()

    def nbr_terms(core, dst):
        @pl.loop(0, 4)
        def _(zz):
            tt = zz * 2 + core
            value = (mm_nt(gkv[tt], wkv[...]) + mm_nt(gvv[tt], wvv[...])).astype(BF)
            dst[zz, 0] = value[:96]
            dst[zz, 1] = value[96:]

    def streamed(left, core, dst, product):
        @pl.loop(0, 4)
        def _(zz):
            value = product(left, zz * 2 + core).astype(BF)
            dst[zz, 0] = value[:192]
            dst[zz, 1] = value[192:]

    def share(n, T, P):
        return remote(T, P, ps.at[n], pr.at[n], (d, me.partner))

    sn, so, sh = share(0, Tn, Pn), share(1, T, Po), share(2, T, Ph)
    for n in range(4, 8):
        loads[n].wait()
    nbr_terms(1 - c, Tn)
    sn.start()
    weights(rq.r1, ro.r1)
    weights(rq.l1, ro.l1)
    rq.second()
    ro.second()
    nbr_terms(c, Un)

    def out_product(left, tt):
        return mm(left[...], W[tt])

    def hid_product(left, tt):
        return mm_nt(left[...], W[tt])

    w_load = [pltpu.make_async_copy(wo.at[:, pl.ds(n * 512, 512)], W.at[n], wload.at[n]) for n in range(8)]
    w_load.append(pltpu.make_async_copy(wq, W, wload.at[8]))
    for n in range(8):
        w_load[n].start()
    sn.wait_recv()

    def merge(U, P):
        @pl.loop(0, 4)
        def _(zz):
            for h in range(2):
                add_into(U.at[zz, h], P.at[zz, h])

    merge(Un, Pn)
    zn.first()
    zn.second()
    for n in range(8):
        w_load[n].wait()
    streamed(attv, 1 - c, T, out_product)
    so.start()
    streamed(attv, c, Uo, out_product)
    w_load[8].start()
    so.wait_recv()
    merge(Uo, Po)
    zo.first()
    zo.second()
    zn.middle()
    rq.middle()
    ro.middle()
    w_load[8].wait()
    so.wait_send()
    streamed(gqv, 1 - c, T, hid_product)
    sh.start()
    streamed(gqv, c, Uh, hid_product)
    sh.wait_recv()
    merge(Uh, Ph)
    zh.first()
    zh.second()
    weights(rq.pos, ro.pos)
    loads[8].wait()

    @pl.loop(0, 7)
    def _(m):
        cols = pl.ds(pl.multiple_of(m * 128, 128), 128)
        left = N[:, :, cols].reshape(1536, 128)
        GK[cols, :] = mm_tn(left, gkv[...].reshape(1536, 512))
        GV[cols, :] = mm_tn(left, gvv[...].reshape(1536, 512))

    @pl.loop(0, 16)
    def _(dd):
        rows = pl.ds(pl.multiple_of(dd * 56, 8), 56)
        value = jnp.concatenate([GK[rows, :], GV[rows, :]], axis=0).astype(BF)
        xx, yy = dd // 4, dd % 4
        Ba[xx, yy // 2, (yy % 2) * 2] = value[:, :128]
        Ba[xx, yy // 2, (yy % 2) * 2 + 1] = value[:, 128:256]
        Bb[yy, xx // 2, (xx % 2) * 2] = value[:, 256:384]
        Bb[yy, xx // 2, (xx % 2) * 2 + 1] = value[:, 384:]

    ra.first()
    rb.first()
    ra.second()
    rb.second()
    zn.arrive()
    for h in range(2):
        value = zn.total(h).astype(BF)
        for k in range(6):
            live[h * 6 + k] = value[k * 16:(k + 1) * 16]
    owners, slots = [], []
    for k in range(12):
        owner = shard_s[k % 2, k // 2]
        position = jnp.int32(0)
        for other in owners:
            position = position + (other == owner).astype(jnp.int32)
        owners.append(owner)
        slots.append(owner * 2 + position)

    def give(n, dst):
        return remote(spread.at[me.peer(n)], ret.at[dst], fs.at[n], fr.at[n], (me.peer(n), t))

    def choose(o, p):
        where = jnp.int32(12)
        for k in range(12):
            where = jnp.where(slots[k] == o * 2 + p, jnp.int32(k), where)
        return where

    @pl.loop(1, 16)
    def _(n):
        o = me.peer(n)
        for p in range(2):
            spread[o, p] = live[choose(o, p)]
        give(n, d).start()

    for p in range(2):
        ret[d, p] = live[choose(d, p)]
    zo.middle()
    zh.middle()
    rq.arrive()
    rq.sum_in_place()
    rq2.first()
    rq2.second()
    ro.arrive()
    ro.sum_in_place()
    ro2.first()
    ro2.second()
    ra.middle()
    rb.middle()
    zo.arrive()
    for h in range(2):
        out_o[h * 192:(h + 1) * 192, :] = zo.total(h).astype(BF)
    zh.arrive()
    for h in range(2):
        hid_o[h * 192:(h + 1) * 192, :] = zh.total(h).astype(BF)
    rq2.middle()
    ro2.middle()
    ra.arrive()
    ra.sum_in_place()
    ra2.first()
    ra2.second()
    rb.arrive()
    rb.sum_in_place()
    rb2.first()
    rb2.second()
    rq2.arrive()
    for h in range(2):
        gq_o[:, h * 256:(h + 1) * 256] = rq2.total(h).T
    ro2.arrive()
    for h in range(2):
        go_o[h * 256:(h + 1) * 256, :] = ro2.total(h)
    ra2.middle()
    rb2.middle()

    @pl.loop(1, 16)
    def _(n):
        give(n, me.source(n)).wait_recv()

    ret_o[...] = ret[...]
    ra2.arrive()
    rb2.arrive()
    for h in range(2):
        for base, one in ((0, ra2), (256, rb2)):
            value = one.total(h)
            low = base + h * 128
            gk_o[:, low:low + 128] = value[:56]
            gv_o[:, low:low + 128] = value[56:]
    for one in (rq, ro, ra, rb, rq2, ro2, ra2, rb2, zo, zh, zn):
        one.sent()
    for one in (sn, sh):
        one.wait_send()

    @pl.loop(1, 16)
    def _(n):
        give(n, d).wait_send()


def reduce_call(nbr_shard, att, gq, gk, gv, h, cc, n, wq, wo, wk, wv):
    S = jax.ShapeDtypeStruct
    V = pltpu.VMEM
    big = [V((4, 2, 4, 256, 256), BF)] * 2 + [V((4, 2, 4, 112, 128), BF)] * 2
    first = []
    for r, w in ((256, 256), (256, 256), (112, 128), (112, 128)):
        first += [V((2, 4, r, w), BF), V((2, 2, 4, r, w), BF)]
    second = []
    for r, w in ((256, 256), (256, 256), (112, 128), (112, 128)):
        second += [V((2, r, w), BF), V((2, 2, r, w), BF)]
    terms = [V((4, 2, 192, 512), BF)] * 5 + [V((4, 2, 96, 896), BF)] * 3
    rings = []
    for r, w in ((192, 512), (192, 512), (96, 896)):
        rings += [V((2, r, w), BF), V((2, 2, r, w), BF)]
    return pl.pallas_call(
        reduce_kernel,
        name="reduce",
        out_shape=(
            S((384, 512), BF), S((384, 512), BF), S((16, 2, 16, 896), BF),
            S((256, 512), F32), S((56, 512), F32), S((56, 512), F32), S((512, 256), F32),
        ),
        in_specs=[SM] + [ANY] * 11,
        out_specs=(VM,) * 7,
        scratch_shapes=[
            V((384, 512), BF), V((384, 512), BF), V((512, 384), BF), V((512, 384), BF),
            V((8, 192, 512), BF), V((8, 192, 512), BF), V((8, 384, 512), BF), V((8, 384, 512), BF),
            V((8, 192, 896), BF), V((8, 512, 512), BF), V((896, 512), BF), V((896, 512), BF),
            V((896, 512), F32), V((896, 512), F32),
        ]
        + big + first + second + terms + rings
        + [
            V((13, 16, 896), BF), V((16, 2, 16, 896), BF), V((16, 2, 16, 896), BF),
            DMA((9,)), DMA((9,)), DMA((3,)), DMA((3,)), DMA((11, 6)), DMA((11, 6)), DMA((16,)), DMA((16,)),
        ],
        compiler_params=pltpu.CompilerParams(
            collective_id=2, has_side_effects=True, vmem_limit_bytes=64 * 2**20 - 2**17
        ),
    )(nbr_shard, att, gq, gk, gv, h, cc, n, wq, wo, wk, wv)


def finish_kernel(want_s, ret, *refs):
    kept, out_ref, given, sems = refs[:6], refs[6], refs[7:13], refs[13]
    copies = [pltpu.make_async_copy(a, b, sems.at[n]) for n, (a, b) in enumerate(zip(kept, given))]
    for one in copies:
        one.start()
    out_ref[...] = jnp.zeros_like(out_ref)

    @pl.loop(0, 32)
    def _(s):
        row = want_s[s]
        out_ref[row] += ret[s // 2, s % 2].astype(F32)

    for one in copies:
        one.wait()


def finish_call(want, ret, kept):
    S = jax.ShapeDtypeStruct
    return pl.pallas_call(
        finish_kernel,
        name="finish",
        out_shape=(S((64, 16, 896), F32),) + tuple(S(a.shape, a.dtype) for a in kept),
        in_specs=[SM] + [VM] * 7,
        out_specs=(VM,) + (ANY,) * 6,
        scratch_shapes=[DMA((6,))],
        compiler_params=pltpu.CompilerParams(vmem_limit_bytes=64 * 2**20 - 2**17),
    )(want, ret, *kept)


def shards(hidden_in, encodings, nbr_shard, nbr_row, w_query, w_key, w_value, w_output, cotangent):
    wq = w_query.reshape(8, 512, 512)
    owners, rows = nbr_shard.T, nbr_row.T
    att, gq, gk, gv, h, c, n, want = gather_call(
        owners, rows, hidden_in, cotangent, encodings, wq, w_output, w_key, w_value
    )
    out, hid, ret, sq, sk, sv, so = reduce_call(
        owners, att, gq, gk, gv, h, c, n, wq, w_output, w_key, w_value
    )
    enc, out, hid, sq, sk, sv, so = finish_call(want, ret, (out, hid, sq, sk, sv, so))
    return (out, hid, enc, sq, sk, sv, so)


def solution(mesh):
    return jax.shard_map(
        shards,
        mesh=mesh,
        in_specs=(
            P("dp", "tensor"),
            P("dp", "tensor", None),
            P("dp", None),
            P("dp", None),
            P(None, "tensor"),
            P(None, "tensor"),
            P(None, "tensor"),
            P("tensor", None),
            P("dp", "tensor"),
        ),
        out_specs=(
            P("dp", "tensor"),
            P("dp", "tensor"),
            P("dp", "tensor", None),
            P("dp", "tensor"),
            P("dp", "tensor"),
            P("dp", "tensor"),
            P("tensor", "dp"),
        ),
        check_vma=False,
    )
```

```python
import math

import jax
import jax.numpy as jnp
from jax import lax
from jax.experimental import pallas as pl
from jax.experimental.pallas import tpu as pltpu
from jax.sharding import PartitionSpec as P

HD = 128
SPAN = 64
NB = 128
K_NBR = 2
MESH = pl.DeviceIdType.MESH
BF = jnp.bfloat16
F32 = jnp.float32
ANY = pl.BlockSpec(memory_space=pl.ANY)
VM = pl.BlockSpec(memory_space=pltpu.VMEM)
SM = pl.BlockSpec(memory_space=pltpu.SMEM)
DMA = pltpu.SemaphoreType.DMA
NT = (((1,), (1,)), ((), ()))
TN = (((0,), (0,)), ((), ()))


def mm(a, b):
    return jnp.dot(a, b, preferred_element_type=F32)


def mm_nt(a, b):
    return lax.dot_general(a, b, NT, preferred_element_type=F32)


def mm_tn(a, b):
    return lax.dot_general(a, b, TN, preferred_element_type=F32)


class Place:
    def __init__(self):
        self.d = lax.axis_index("dp")
        self.t = lax.axis_index("tensor")
        self.x, self.y = self.d // 4, self.d % 4
        self.z, self.c = self.t // 2, self.t % 2
        self.partner = self.z * 2 + (1 - self.c)
        self.tr = ((self.z + 1) % 4) * 2 + self.c
        self.tl = ((self.z + 3) % 4) * 2 + self.c
        self.tf = ((self.z + 2) % 4) * 2 + self.c

    def peer(self, n):
        return (self.d + n) % 16

    def source(self, n):
        return (self.d + 16 - n) % 16

    def greet(self):
        barrier = pltpu.get_barrier_semaphore()
        for other in (self.partner, self.tr, self.tl):
            pl.semaphore_signal(barrier, inc=1, device_id=(self.d, other), device_id_type=MESH)

        @pl.loop(1, 16)
        def _(n):
            pl.semaphore_signal(barrier, inc=1, device_id=(self.peer(n), self.t), device_id_type=MESH)

        pl.semaphore_wait(barrier, 18)


def remote(src, dst, send, recv, dev):
    return pltpu.make_async_remote_copy(
        src_ref=src, dst_ref=dst, send_sem=send, recv_sem=recv, device_id=dev, device_id_type=MESH
    )


class Gather:
    def __init__(self, me, buf, half, send, recv):
        self.me, self.buf, self.half, self.send, self.recv = me, buf, half, send, recv

    def copy(self, n, t, dev, part=None):
        view = self.buf.at[t] if part is None else self.buf.at[t, pl.ds(part * self.half, self.half)]
        return remote(view, view, self.send.at[n], self.recv.at[n], (self.me.d, dev))

    def start(self):
        me = self.me
        self.copy(0, me.t, me.tr).start()
        self.copy(1, me.t, me.tl).start()
        self.copy(4, me.t, me.partner).start()

    def forward(self):
        me = self.me
        self.copy(0, me.tl, me.tr).wait_recv()
        self.copy(2, me.tl, me.tr, 0).start()
        self.copy(5, me.tl, me.partner).start()
        self.copy(1, me.tr, me.tl).wait_recv()
        self.copy(3, me.tr, me.tl, 1).start()
        self.copy(6, me.tr, me.partner).start()

    def far(self):
        me = self.me
        self.copy(2, me.tf, me.tr, 0).wait_recv()
        self.copy(3, me.tf, me.tl, 1).wait_recv()
        self.copy(7, me.tf, me.partner).start()

    def other(self, t):
        return t + 1 - 2 * self.me.c

    def near_pairs(self):
        me = self.me
        for n, t in ((4, me.t), (5, me.tl), (6, me.tr)):
            self.copy(n, self.other(t), me.partner).wait_recv()

    def last_pair(self):
        self.copy(7, self.other(self.me.tf), self.me.partner).wait_recv()

    def pairs(self):
        self.near_pairs()
        self.last_pair()

    def sent(self):
        me = self.me
        self.copy(0, me.t, me.tr).wait_send()
        self.copy(1, me.t, me.tl).wait_send()
        self.copy(2, me.tl, me.tr, 0).wait_send()
        self.copy(3, me.tr, me.tl, 1).wait_send()
        for n, t in ((4, me.t), (5, me.tl), (6, me.tr), (7, me.tf)):
            self.copy(n, t, me.partner).wait_send()


def attend(q_ref, ga_ref, k_ref, v_ref, att_ref, gq_ref, gk_ref, gv_ref, rows, keys):
    scale = 1.0 / math.sqrt(HD)
    heads = [slice(h * HD, (h + 1) * HD) for h in range(4)]
    q, ga = [q_ref[rows, c] for c in heads], [ga_ref[rows, c] for c in heads]
    k = [k_ref[:, keys, c].reshape(256, HD) for c in heads]
    v = [v_ref[:, keys, c].reshape(256, HD) for c in heads]
    s = [mm_nt(a, b) * scale for a, b in zip(q, k)]
    gp = [mm_nt(a, b) for a, b in zip(ga, v)]
    e = [jnp.exp(a - jnp.max(a, axis=-1, keepdims=True)) for a in s]
    p = [a * (1.0 / jnp.sum(a, axis=-1, keepdims=True)) for a in e]
    pb = [a.astype(BF) for a in p]
    inner = [jnp.sum(a * b, axis=-1, keepdims=True) for a, b in zip(gp, p)]
    gs = [(a * (b - c) * scale).astype(BF) for a, b, c in zip(p, gp, inner)]
    for n, c in enumerate(heads):
        att_ref[rows, c] = mm(pb[n], v[n]).astype(BF)
        gq_ref[rows, c] = mm(gs[n], k[n]).astype(BF)
    for n, c in enumerate(heads):
        gv_ref[:, keys, c] = mm_tn(pb[n], ga[n]).astype(BF).reshape(8, 32, HD)
        gk_ref[:, keys, c] = mm_tn(gs[n], q[n]).astype(BF).reshape(8, 32, HD)


class Ring:
    def __init__(self, group, f1, f2, send, recv, pos, right, left):
        self.group, self.f1, self.f2 = group, f1, f2
        self.pos = pos
        self.r1, self.r2, self.l1 = (pos + 1) % 4, (pos + 2) % 4, (pos + 3) % 4

        def cp(n, src, dst, dev):
            return remote(src, dst, send.at[n], recv.at[n], dev)

        self.s = [
            cp(0, group(self.r2, 0), f1.at[0], right),
            cp(1, group(self.r2, 1), f1.at[1], left),
            cp(2, group(self.r1, 1), f2.at[0, 1], right),
            cp(3, group(self.l1, 0), f2.at[1, 0], left),
            cp(4, group(self.r1, 0), f2.at[0, 0], right),
            cp(5, group(self.l1, 1), f2.at[1, 1], left),
        ]

    def first(self):
        self.s[0].start()
        self.s[1].start()

    def second(self):
        self.s[2].start()
        self.s[3].start()

    def middle(self):
        self.s[0].wait_recv()
        add_into(self.group(self.r1, 0), self.f1.at[0])
        self.s[4].start()
        self.s[1].wait_recv()
        add_into(self.group(self.l1, 1), self.f1.at[1])
        self.s[5].start()

    def arrive(self):
        for n in range(2, 6):
            self.s[n].wait_recv()

    def sum_in_place(self):
        for h in range(2):
            add_into(self.group(self.pos, h), self.f2.at[0, h], self.f2.at[1, h])

    def total(self, h):
        return (
            self.group(self.pos, h)[...].astype(F32)
            + self.f2[0, h].astype(F32)
            + self.f2[1, h].astype(F32)
        )

    def sent(self):
        for n in range(6):
            self.s[n].wait_send()


def add_into(dst, *srcs):
    lead, rows = dst.shape[:-2], dst.shape[-2]
    step = 32 if rows % 32 == 0 else 16

    def part(*where):
        value = dst[where].astype(F32)
        for src in srcs:
            value = value + src[where].astype(F32)
        dst[where] = value.astype(BF)

    if lead:

        @pl.loop(0, lead[0])
        def _(q):
            @pl.loop(0, rows // step)
            def _(r):
                part(q, pl.ds(pl.multiple_of(r * step, step), step))
    else:

        @pl.loop(0, rows // step)
        def _(r):
            part(pl.ds(pl.multiple_of(r * step, step), step))


def layer_kernel(
    shard_s, row_s, hid, cot, enc, wq, wo, wk, wv,
    want_o, out_o, hid_o, ret_o, gq_o, gk_o, gv_o, go_o,
    qv, gav, kv, vv, H, C, N, encv, outg, arr, req, wanted, want_s, wqv, wov, wkv, wvv,
    attv, gqv, gkv, gvv, attT, gqT, GK, GV,
    Bq, Bo, Ba, Bb, q1, q2, o1, o2, a1, a2, b1, b2, q3, q4, o3, o4, a3, a4, b3, b4,
    Po, Ph, Pn, zo1, zo2, zh1, zh2, zn1, zn2, ret,
    load, zs, zr, rs, rr, fs, fr, ps, pr, ss, sr, bs, br,
):
    me = Place()
    d, t = me.d, me.t
    loads = [
        pltpu.make_async_copy(hid, H.at[t], load.at[0]),
        pltpu.make_async_copy(cot, C.at[t], load.at[1]),
        pltpu.make_async_copy(enc, encv, load.at[2]),
        pltpu.make_async_copy(wq, wqv, load.at[3]),
        pltpu.make_async_copy(wo, wov, load.at[4]),
        pltpu.make_async_copy(wk, wkv, load.at[5]),
        pltpu.make_async_copy(wv, wvv, load.at[6]),
    ]
    for one in loads:
        one.start()
    owners, slots = [], []
    lane = lax.broadcasted_iota(jnp.int32, (8, 128), 1)
    table = jnp.full((8, 128), 0, jnp.int32)
    for k in range(12):
        owner = shard_s[k % 2, k // 2]
        position = jnp.int32(0)
        for other in owners:
            position = position + (other == owner).astype(jnp.int32)
        owners.append(owner)
        slots.append((owner, jnp.minimum(position, 1)))
        table = jnp.where(lane == owner * 2 + position, row_s[k % 2, k // 2], table)
    req[...] = table
    wanted[d] = table
    me.greet()

    def request(n, dst):
        return remote(req, wanted.at[dst], rs.at[n], rr.at[n], (me.peer(n), t))

    @pl.loop(1, 16)
    def _(n):
        request(n, d).start()

    gh = Gather(me, H, 192, zs.at[0], zr.at[0])
    gc = Gather(me, C, 192, zs.at[1], zr.at[1])
    gn = Gather(me, N, 96, zs.at[2], zr.at[2])
    loads[0].wait()
    gh.start()
    loads[1].wait()
    gc.start()
    loads[2].wait()

    @pl.loop(1, 16)
    def _(n):
        request(n, me.source(n)).wait_recv()

    to_s = pltpu.make_async_copy(wanted, want_s, load.at[7])
    to_s.start()
    to_s.wait()

    def fetch(n, dst):
        return remote(outg.at[me.peer(n)], arr.at[dst], fs.at[n], fr.at[n], (me.peer(n), t))

    @pl.loop(1, 16)
    def _(n):
        reader = me.peer(n)
        for p in range(2):
            outg[reader, p] = encv[want_s[reader, 0, d * 2 + p]]
        fetch(n, d).start()

    for p in range(2):
        arr[d, p] = encv[want_s[d, 0, d * 2 + p]]
    gh.forward()

    @pl.loop(1, 16)
    def _(n):
        fetch(n, me.source(n)).wait_recv()

    for k in range(12):
        owner, position = slots[k]
        N[t, k * 16:(k + 1) * 16, :] = arr[owner, position]
    gn.start()
    gc.forward()
    gh.far()
    for r in range(16):
        for p in range(2):
            want_o[r * 2 + p] = want_s[r, 0, d * 2 + p]
    loads[3].wait()
    gh.pairs()

    @pl.loop(0, 2)
    def _(m):
        cols = pl.ds(pl.multiple_of(m * 256, 256), 256)
        value = mm(H[0], wqv[0, :, cols])
        for k in range(1, 8):
            value = value + mm(H[k], wqv[k, :, cols])
        qv[:, cols] = value.astype(BF)

    gn.forward()
    loads[4].wait()
    loads[5].wait()
    loads[6].wait()

    def project(k):
        kv[k] = mm(N[k], wkv[...]).astype(BF)
        vv[k] = mm(N[k], wvv[...]).astype(BF)

    @pl.loop(0, 3)
    def _(s):
        project((me.z + (s + 3)) % 4 * 2 + me.c)

    gc.far()
    gn.near_pairs()

    @pl.loop(0, 3)
    def _(s):
        project((me.z + (s + 3)) % 4 * 2 + 1 - me.c)

    gc.pairs()
    gn.far()

    @pl.loop(0, 2)
    def _(m):
        cols = pl.ds(pl.multiple_of(m * 256, 256), 256)
        value = mm_nt(C[0], wov[cols, 0:512])
        for k in range(1, 8):
            value = value + mm_nt(C[k], wov[cols, k * 512:(k + 1) * 512])
        gav[:, cols] = value.astype(BF)

    project(me.tf)
    gn.last_pair()
    project((me.z + 2) % 4 * 2 + 1 - me.c)

    @pl.loop(0, 6, unroll=2)
    def _(s):
        rows = pl.ds(pl.multiple_of(s * 64, 64), 64)
        keys = pl.ds(pl.multiple_of(s * 32, 32), 32)
        attend(qv, gav, kv, vv, attv, gqv, gkv, gvv, rows, keys)

    @pl.loop(1, 16)
    def _(n):
        request(n, d).wait_send()
        fetch(n, d).wait_send()

    right_x = ((me.x + 1) % 4 * 4 + me.y, t)
    left_x = ((me.x + 3) % 4 * 4 + me.y, t)
    right_y = (me.x * 4 + (me.y + 1) % 4, t)
    left_y = (me.x * 4 + (me.y + 3) % 4, t)
    right_z, left_z = (d, me.tr), (d, me.tl)
    along = {"x": (me.x, right_x, left_x), "y": (me.y, right_y, left_y), "z": (me.z, right_z, left_z)}

    def ring(n, group, f1, f2, axis):
        return Ring(group, f1, f2, ss.at[n], sr.at[n], *along[axis])

    def pair(n, buf, f1, f2, f3, f4, first, second):
        mine = along[first][0]
        one = ring(n, lambda g, h: buf.at[g, h], f1, f2, first)
        two = ring(n + 1, lambda g, h: buf.at[mine, g // 2, (g % 2) * 2 + h], f3, f4, second)
        return one, two

    rq, rq2 = pair(0, Bq, q1, q2, q3, q4, "x", "y")
    ro, ro2 = pair(2, Bo, o1, o2, o3, o4, "y", "x")
    ra, ra2 = pair(4, Ba, a1, a2, a3, a4, "x", "y")
    rb, rb2 = pair(6, Bb, b1, b2, b3, b4, "y", "x")
    zo = ring(8, lambda g, h: H.at[g, pl.ds(h * 192, 192)], zo1, zo2, "z")
    zh = ring(9, lambda g, h: H.at[4 + g, pl.ds(h * 192, 192)], zh1, zh2, "z")
    zn = ring(10, lambda g, h: N.at[4 + g, pl.ds(h * 96, 96)], zn1, zn2, "z")

    attT[...] = attv[...].T
    gqT[...] = gqv[...].T

    def weights(group_x, group_y):
        @pl.loop(0, 4)
        def _(s):
            dq = group_x * 4 + s
            do = s * 4 + group_y
            value = mm(gqT[...], H[dq // 2, :, pl.ds(pl.multiple_of((dq % 2) * 256, 256), 256)]).astype(BF)
            Bq[group_x, s // 2, (s % 2) * 2] = value[:256]
            Bq[group_x, s // 2, (s % 2) * 2 + 1] = value[256:]
            value = mm(attT[...], C[do // 2, :, pl.ds(pl.multiple_of((do % 2) * 256, 256), 256)]).astype(BF)
            Bo[group_y, s // 2, (s % 2) * 2] = value[:256]
            Bo[group_y, s // 2, (s % 2) * 2 + 1] = value[256:]

    weights(rq.r2, ro.r2)
    rq.first()
    ro.first()
    weights(rq.r1, ro.r1)
    weights(rq.l1, ro.l1)
    rq.second()
    ro.second()
    weights(rq.pos, ro.pos)
    for low, B in ((0, Ba), (256, Bb)):

        @pl.loop(0, 7)
        def _(m):
            cols = pl.ds(pl.multiple_of(m * 128, 128), 128)
            left = N[:, :, cols].reshape(1536, 128)
            GK[cols, :] = mm_tn(left, gkv[:, :, low:low + 256].reshape(1536, 256))
            GV[cols, :] = mm_tn(left, gvv[:, :, low:low + 256].reshape(1536, 256))

        @pl.loop(0, 16)
        def _(dd):
            rows = pl.ds(pl.multiple_of(dd * 56, 8), 56)
            value = jnp.concatenate([GK[rows, :], GV[rows, :]], axis=0).astype(BF)
            one, two = (dd // 4, dd % 4) if low == 0 else (dd % 4, dd // 4)
            B[one, two // 2, (two % 2) * 2] = value[:, :128]
            B[one, two // 2, (two % 2) * 2 + 1] = value[:, 128:]

    ra.first()
    rb.first()
    ra.second()
    rb.second()
    gn.sent()

    def terms(buf, base, core, product):
        @pl.loop(0, 4)
        def _(zz):
            buf[base + zz] = product(zz * 2 + core).astype(BF)

    def nbr_product(tt):
        return mm_nt(gkv[tt], wkv[...]) + mm_nt(gvv[tt], wvv[...])

    def out_product(tt):
        return mm(attv[...], wov[:, pl.ds(pl.multiple_of(tt * 512, 512), 512)])

    def hid_product(tt):
        return mm_nt(gqv[...], wqv[tt])

    def share(n, buf, base, P):
        return remote(buf.at[pl.ds(base, 4)], P, ps.at[n], pr.at[n], (d, me.partner))

    sn, so, sh = share(0, N, 0, Pn), share(1, C, 0, Po), share(2, C, 4, Ph)

    def merge(buf, base, P):
        @pl.loop(0, 4)
        def _(zz):
            add_into(buf.at[base + zz], P.at[zz])

    terms(N, 0, 1 - me.c, nbr_product)
    sn.start()
    terms(N, 4, me.c, nbr_product)
    sn.wait_recv()
    merge(N, 4, Pn)
    zn.first()
    zn.second()
    gh.sent()
    gc.sent()
    terms(C, 0, 1 - me.c, out_product)
    so.start()
    terms(H, 0, me.c, out_product)
    so.wait_recv()
    merge(H, 0, Po)
    zo.first()
    zo.second()
    rq.middle()
    ro.middle()
    zn.middle()
    terms(C, 4, 1 - me.c, hid_product)
    sh.start()
    terms(H, 4, me.c, hid_product)
    sh.wait_recv()
    merge(H, 4, Ph)
    zh.first()
    zh.second()
    zn.arrive()
    for h in range(2):
        value = zn.total(h).astype(BF)
        for k in range(6):
            encv[32 + h * 6 + k] = value[k * 16:(k + 1) * 16]
    encv[44] = jnp.zeros((16, 896), BF)
    def give(n, dst):
        return remote(encv.at[pl.ds(me.peer(n) * 2, 2)], ret.at[dst], bs.at[n], br.at[n], (me.peer(n), t))

    def choose(o, p):
        where = jnp.int32(12)
        for k in range(12):
            where = jnp.where(slots[k][0] * 2 + slots[k][1] == o * 2 + p, jnp.int32(k), where)
        return where

    @pl.loop(1, 16)
    def _(n):
        o = me.peer(n)
        for p in range(2):
            encv[o * 2 + p] = encv[32 + choose(o, p)]
        give(n, d).start()

    for p in range(2):
        ret[d, p] = encv[32 + choose(d, p)]
    zo.middle()
    zh.middle()
    rq.arrive()
    rq.sum_in_place()
    rq2.first()
    rq2.second()
    ro.arrive()
    ro.sum_in_place()
    ro2.first()
    ro2.second()
    ra.middle()
    rb.middle()
    zo.arrive()
    for h in range(2):
        out_o[h * 192:(h + 1) * 192, :] = zo.total(h).astype(BF)
    zh.arrive()
    for h in range(2):
        hid_o[h * 192:(h + 1) * 192, :] = zh.total(h).astype(BF)
    rq2.middle()
    ro2.middle()
    ra.arrive()
    ra.sum_in_place()
    ra2.first()
    ra2.second()
    rb.arrive()
    rb.sum_in_place()
    rb2.first()
    rb2.second()
    rq2.arrive()
    for h in range(2):
        gq_o[:, h * 256:(h + 1) * 256] = rq2.total(h).T
    ro2.arrive()
    for h in range(2):
        go_o[h * 256:(h + 1) * 256, :] = ro2.total(h)
    ra2.middle()
    rb2.middle()

    @pl.loop(1, 16)
    def _(n):
        give(n, me.source(n)).wait_recv()

    back = pltpu.make_async_copy(ret, ret_o, load.at[8])
    back.start()
    ra2.arrive()
    rb2.arrive()
    for h in range(2):
        for base, one in ((0, ra2), (256, rb2)):
            value = one.total(h)
            low = base + h * 128
            gk_o[:, low:low + 128] = value[:56]
            gv_o[:, low:low + 128] = value[56:]
    for one in (rq, ro, ra, rb, rq2, ro2, ra2, rb2, zo, zh, zn):
        one.sent()
    back.wait()
    for one in (sn, so, sh):
        one.wait_send()

    @pl.loop(1, 16)
    def _(n):
        give(n, d).wait_send()


def layer_call(nbr_shard, nbr_row, hidden_in, cotangent, encodings, wq, wo, wk, wv):
    S = jax.ShapeDtypeStruct
    V = pltpu.VMEM
    tok, nbr, wide = V((384, 512), BF), V((8, 192, 512), BF), V((512, 384), BF)
    sizes = ((256, 256), (256, 256), (112, 128), (112, 128))
    big = [V((4, 2, 4, r, w), BF) for r, w in sizes]
    first, second, rings = [], [], []
    for r, w in sizes:
        first += [V((2, 4, r, w), BF), V((2, 2, 4, r, w), BF)]
        second += [V((2, r, w), BF), V((2, 2, r, w), BF)]
    for r, w in ((192, 512), (192, 512), (96, 896)):
        rings += [V((2, r, w), BF), V((2, 2, r, w), BF)]
    return pl.pallas_call(
        layer_kernel,
        name="layer",
        out_shape=(
            S((32,), jnp.int32), S((384, 512), BF), S((384, 512), BF), S((16, 2, 16, 896), BF),
            S((256, 512), F32), S((56, 512), F32), S((56, 512), F32), S((512, 256), F32),
        ),
        in_specs=[SM, SM] + [ANY] * 7,
        out_specs=(SM, VM, VM, ANY, VM, VM, VM, VM),
        scratch_shapes=[
            tok, tok, nbr, nbr,
            V((8, 384, 512), BF), V((8, 384, 512), BF), V((8, 192, 896), BF),
            V((64, 16, 896), BF), V((16, 2, 16, 896), BF), V((16, 2, 16, 896), BF),
            V((8, 128), jnp.int32), V((16, 8, 128), jnp.int32), pltpu.SMEM((16, 8, 128), jnp.int32),
            V((8, 512, 512), BF), V((512, 4096), BF), V((896, 512), BF), V((896, 512), BF),
            tok, tok, nbr, nbr, wide, wide, V((896, 256), F32), V((896, 256), F32),
        ]
        + big + first + second
        + [V((4, 384, 512), BF), V((4, 384, 512), BF), V((4, 192, 896), BF)]
        + rings
        + [
            V((16, 2, 16, 896), BF),
            DMA((9,)), DMA((3, 8)), DMA((3, 8)), DMA((16,)), DMA((16,)), DMA((16,)), DMA((16,)),
            DMA((3,)), DMA((3,)), DMA((11, 6)), DMA((11, 6)), DMA((16,)), DMA((16,)),
        ],
        compiler_params=pltpu.CompilerParams(
            collective_id=1, has_side_effects=True, vmem_limit_bytes=64 * 2**20 - 2**17
        ),
    )(nbr_shard, nbr_row, hidden_in, cotangent, encodings, wq, wo, wk, wv)


def finish_kernel(want_s, ret, *refs):
    kept, out_ref, given, sems = refs[:6], refs[6], refs[7:13], refs[13]
    copies = [pltpu.make_async_copy(a, b, sems.at[n]) for n, (a, b) in enumerate(zip(kept, given))]
    for one in copies:
        one.start()
    out_ref[...] = jnp.zeros_like(out_ref)

    @pl.loop(0, 32)
    def _(s):
        row = want_s[s]
        out_ref[row] += ret[s // 2, s % 2].astype(F32)

    for one in copies:
        one.wait()


def finish_call(want, ret, kept):
    S = jax.ShapeDtypeStruct
    return pl.pallas_call(
        finish_kernel,
        name="finish",
        out_shape=(S((64, 16, 896), F32),) + tuple(S(a.shape, a.dtype) for a in kept),
        in_specs=[SM] + [VM] * 7,
        out_specs=(VM,) + (ANY,) * 6,
        scratch_shapes=[DMA((6,))],
        compiler_params=pltpu.CompilerParams(vmem_limit_bytes=64 * 2**20 - 2**17),
    )(want, ret, *kept)


def shards(hidden_in, encodings, nbr_shard, nbr_row, w_query, w_key, w_value, w_output, cotangent):
    wq = w_query.reshape(8, 512, 512)
    owners, rows = nbr_shard.T, nbr_row.T
    want, out, hid, ret, sq, sk, sv, so = layer_call(
        owners, rows, hidden_in, cotangent, encodings, wq, w_output, w_key, w_value
    )
    enc, out, hid, sq, sk, sv, so = finish_call(want, ret, (out, hid, sq, sk, sv, so))
    return (out, hid, enc, sq, sk, sv, so)


def solution(mesh):
    return jax.shard_map(
        shards,
        mesh=mesh,
        in_specs=(
            P("dp", "tensor"),
            P("dp", "tensor", None),
            P("dp", None),
            P("dp", None),
            P(None, "tensor"),
            P(None, "tensor"),
            P(None, "tensor"),
            P("tensor", None),
            P("dp", "tensor"),
        ),
        out_specs=(
            P("dp", "tensor"),
            P("dp", "tensor"),
            P("dp", "tensor", None),
            P("dp", "tensor"),
            P("dp", "tensor"),
            P("dp", "tensor"),
            P("tensor", "dp"),
        ),
        check_vma=False,
    )
```

```python
import math

import jax
import jax.numpy as jnp
from jax import lax
from jax.experimental import pallas as pl
from jax.experimental.pallas import tpu as pltpu
from jax.sharding import PartitionSpec as P

HD = 128
SPAN = 64
NB = 128
K_NBR = 2
MESH = pl.DeviceIdType.MESH
BF = jnp.bfloat16
F32 = jnp.float32
ANY = pl.BlockSpec(memory_space=pl.ANY)
VM = pl.BlockSpec(memory_space=pltpu.VMEM)
SM = pl.BlockSpec(memory_space=pltpu.SMEM)
DMA = pltpu.SemaphoreType.DMA
NT = (((1,), (1,)), ((), ()))
TN = (((0,), (0,)), ((), ()))


def mm(a, b):
    return jnp.dot(a, b, preferred_element_type=F32)


def mm_nt(a, b):
    return lax.dot_general(a, b, NT, preferred_element_type=F32)


def mm_tn(a, b):
    return lax.dot_general(a, b, TN, preferred_element_type=F32)


class Place:
    def __init__(self):
        self.d = lax.axis_index("dp")
        self.t = lax.axis_index("tensor")
        self.x, self.y = self.d // 4, self.d % 4
        self.z, self.c = self.t // 2, self.t % 2
        self.partner = self.z * 2 + (1 - self.c)
        self.tr = ((self.z + 1) % 4) * 2 + self.c
        self.tl = ((self.z + 3) % 4) * 2 + self.c
        self.tf = ((self.z + 2) % 4) * 2 + self.c

    def peer(self, n):
        return (self.d + n) % 16

    def source(self, n):
        return (self.d + 16 - n) % 16

    def greet(self):
        barrier = pltpu.get_barrier_semaphore()
        for other in (self.partner, self.tr, self.tl):
            pl.semaphore_signal(barrier, inc=1, device_id=(self.d, other), device_id_type=MESH)

        @pl.loop(1, 16)
        def _(n):
            pl.semaphore_signal(barrier, inc=1, device_id=(self.peer(n), self.t), device_id_type=MESH)

        pl.semaphore_wait(barrier, 18)


def remote(src, dst, send, recv, dev):
    return pltpu.make_async_remote_copy(
        src_ref=src, dst_ref=dst, send_sem=send, recv_sem=recv, device_id=dev, device_id_type=MESH
    )


class Gather:
    def __init__(self, me, buf, half, send, recv):
        self.me, self.buf, self.half, self.send, self.recv = me, buf, half, send, recv

    def copy(self, n, t, dev, part=None):
        view = self.buf.at[t] if part is None else self.buf.at[t, pl.ds(part * self.half, self.half)]
        return remote(view, view, self.send.at[n], self.recv.at[n], (self.me.d, dev))

    def start(self):
        me = self.me
        self.copy(0, me.t, me.tr).start()
        self.copy(1, me.t, me.tl).start()
        self.copy(4, me.t, me.partner).start()

    def forward(self):
        me = self.me
        self.copy(0, me.tl, me.tr).wait_recv()
        self.copy(2, me.tl, me.tr, 0).start()
        self.copy(5, me.tl, me.partner).start()
        self.copy(1, me.tr, me.tl).wait_recv()
        self.copy(3, me.tr, me.tl, 1).start()
        self.copy(6, me.tr, me.partner).start()

    def far(self):
        me = self.me
        self.copy(2, me.tf, me.tr, 0).wait_recv()
        self.copy(3, me.tf, me.tl, 1).wait_recv()
        self.copy(7, me.tf, me.partner).start()

    def other(self, t):
        return t + 1 - 2 * self.me.c

    def near_pairs(self):
        me = self.me
        for n, t in ((4, me.t), (5, me.tl), (6, me.tr)):
            self.copy(n, self.other(t), me.partner).wait_recv()

    def last_pair(self):
        self.copy(7, self.other(self.me.tf), self.me.partner).wait_recv()

    def pairs(self):
        self.near_pairs()
        self.last_pair()

    def sent(self):
        me = self.me
        self.copy(0, me.t, me.tr).wait_send()
        self.copy(1, me.t, me.tl).wait_send()
        self.copy(2, me.tl, me.tr, 0).wait_send()
        self.copy(3, me.tr, me.tl, 1).wait_send()
        for n, t in ((4, me.t), (5, me.tl), (6, me.tr), (7, me.tf)):
            self.copy(n, t, me.partner).wait_send()


def attend(q_ref, ga_ref, k_ref, v_ref, att_ref, gq_ref, gk_ref, gv_ref, rows, keys):
    scale = 1.0 / math.sqrt(HD)
    heads = [slice(h * HD, (h + 1) * HD) for h in range(4)]
    q, ga = [q_ref[rows, c] for c in heads], [ga_ref[rows, c] for c in heads]
    k = [k_ref[:, keys, c].reshape(256, HD) for c in heads]
    v = [v_ref[:, keys, c].reshape(256, HD) for c in heads]
    s = [mm_nt(a, b) * scale for a, b in zip(q, k)]
    gp = [mm_nt(a, b) for a, b in zip(ga, v)]
    e = [jnp.exp(a - jnp.max(a, axis=-1, keepdims=True)) for a in s]
    p = [a * (1.0 / jnp.sum(a, axis=-1, keepdims=True)) for a in e]
    pb = [a.astype(BF) for a in p]
    inner = [jnp.sum(a * b, axis=-1, keepdims=True) for a, b in zip(gp, p)]
    gs = [(a * (b - c) * scale).astype(BF) for a, b, c in zip(p, gp, inner)]
    for n, c in enumerate(heads):
        att_ref[rows, c] = mm(pb[n], v[n]).astype(BF)
        gq_ref[rows, c] = mm(gs[n], k[n]).astype(BF)
    for n, c in enumerate(heads):
        gv_ref[:, keys, c] = mm_tn(pb[n], ga[n]).astype(BF).reshape(8, 32, HD)
        gk_ref[:, keys, c] = mm_tn(gs[n], q[n]).astype(BF).reshape(8, 32, HD)


class Ring:
    def __init__(self, group, f1, f2, send, recv, pos, right, left):
        self.group, self.f1, self.f2 = group, f1, f2
        self.pos = pos
        self.r1, self.r2, self.l1 = (pos + 1) % 4, (pos + 2) % 4, (pos + 3) % 4

        def cp(n, src, dst, dev):
            return remote(src, dst, send.at[n], recv.at[n], dev)

        self.s = [
            cp(0, group(self.r2, 0), f1.at[0], right),
            cp(1, group(self.r2, 1), f1.at[1], left),
            cp(2, group(self.r1, 1), f2.at[0, 1], right),
            cp(3, group(self.l1, 0), f2.at[1, 0], left),
            cp(4, group(self.r1, 0), f2.at[0, 0], right),
            cp(5, group(self.l1, 1), f2.at[1, 1], left),
        ]

    def first(self):
        self.s[0].start()
        self.s[1].start()

    def second(self):
        self.s[2].start()
        self.s[3].start()

    def middle(self):
        self.s[0].wait_recv()
        add_into(self.group(self.r1, 0), self.f1.at[0])
        self.s[4].start()
        self.s[1].wait_recv()
        add_into(self.group(self.l1, 1), self.f1.at[1])
        self.s[5].start()

    def arrive(self):
        for n in range(2, 6):
            self.s[n].wait_recv()

    def sum_in_place(self):
        for h in range(2):
            add_into(self.group(self.pos, h), self.f2.at[0, h], self.f2.at[1, h])

    def total(self, h):
        return (
            self.group(self.pos, h)[...].astype(F32)
            + self.f2[0, h].astype(F32)
            + self.f2[1, h].astype(F32)
        )

    def sent(self):
        for n in range(6):
            self.s[n].wait_send()


def add_into(dst, *srcs):
    lead, rows = dst.shape[:-2], dst.shape[-2]
    step = 32 if rows % 32 == 0 else 16

    def part(*where):
        value = dst[where].astype(F32)
        for src in srcs:
            value = value + src[where].astype(F32)
        dst[where] = value.astype(BF)

    if lead:

        @pl.loop(0, lead[0])
        def _(q):
            @pl.loop(0, rows // step)
            def _(r):
                part(q, pl.ds(pl.multiple_of(r * step, step), step))
    else:

        @pl.loop(0, rows // step)
        def _(r):
            part(pl.ds(pl.multiple_of(r * step, step), step))


def layer_kernel(
    shard_s, row_s, hid, cot, enc, wq, wo, wk, wv,
    want_o, out_h, hid_h, ret_o, gq_h, gk_h, gv_h, go_h,
    out_o, hid_o, gq_o, gk_o, gv_o, go_o,
    qv, gav, kv, vv, H, C, N, encv, outg, arr, req, wanted, want_s, wqv, wov, wkv, wvv,
    attv, gqv, gkv, gvv, attT, gqT, GK, GV,
    Bq, Bo, Ba, Bb, q1, q2, o1, o2, a1, a2, b1, b2, q3, q4, o3, o4, a3, a4, b3, b4,
    Po, Ph, Pn, zo1, zo2, zh1, zh2, zn1, zn2, ret,
    load, zs, zr, rs, rr, fs, fr, ps, pr, ss, sr, bs, br, keep,
):
    me = Place()
    d, t = me.d, me.t
    loads = [
        pltpu.make_async_copy(hid, H.at[t], load.at[0]),
        pltpu.make_async_copy(cot, C.at[t], load.at[1]),
        pltpu.make_async_copy(enc, encv, load.at[2]),
        pltpu.make_async_copy(wq, wqv, load.at[3]),
        pltpu.make_async_copy(wo, wov, load.at[4]),
        pltpu.make_async_copy(wk, wkv, load.at[5]),
        pltpu.make_async_copy(wv, wvv, load.at[6]),
    ]
    for one in loads:
        one.start()
    owners, slots = [], []
    lane = lax.broadcasted_iota(jnp.int32, (8, 128), 1)
    table = jnp.full((8, 128), 0, jnp.int32)
    for k in range(12):
        owner = shard_s[k % 2, k // 2]
        position = jnp.int32(0)
        for other in owners:
            position = position + (other == owner).astype(jnp.int32)
        owners.append(owner)
        slots.append((owner, jnp.minimum(position, 1)))
        table = jnp.where(lane == owner * 2 + position, row_s[k % 2, k // 2], table)
    req[...] = table
    wanted[d] = table
    me.greet()

    def request(n, dst):
        return remote(req, wanted.at[dst], rs.at[n], rr.at[n], (me.peer(n), t))

    @pl.loop(1, 16)
    def _(n):
        request(n, d).start()

    gh = Gather(me, H, 192, zs.at[0], zr.at[0])
    gc = Gather(me, C, 192, zs.at[1], zr.at[1])
    gn = Gather(me, N, 96, zs.at[2], zr.at[2])
    loads[0].wait()
    gh.start()
    loads[1].wait()
    gc.start()
    loads[2].wait()

    @pl.loop(1, 16)
    def _(n):
        request(n, me.source(n)).wait_recv()

    to_s = pltpu.make_async_copy(wanted, want_s, load.at[7])
    to_s.start()
    to_s.wait()

    def fetch(n, dst):
        return remote(outg.at[me.peer(n)], arr.at[dst], fs.at[n], fr.at[n], (me.peer(n), t))

    @pl.loop(1, 16)
    def _(n):
        reader = me.peer(n)
        for p in range(2):
            outg[reader, p] = encv[want_s[reader, 0, d * 2 + p]]
        fetch(n, d).start()

    for p in range(2):
        arr[d, p] = encv[want_s[d, 0, d * 2 + p]]
    gh.forward()

    @pl.loop(1, 16)
    def _(n):
        fetch(n, me.source(n)).wait_recv()

    for k in range(12):
        owner, position = slots[k]
        N[t, k * 16:(k + 1) * 16, :] = arr[owner, position]
    gn.start()
    gc.forward()
    gh.far()
    for r in range(16):
        for p in range(2):
            want_o[r * 2 + p] = want_s[r, 0, d * 2 + p]
    loads[3].wait()
    gh.pairs()

    @pl.loop(0, 2)
    def _(m):
        cols = pl.ds(pl.multiple_of(m * 256, 256), 256)
        value = mm(H[0], wqv[0, :, cols])
        for k in range(1, 8):
            value = value + mm(H[k], wqv[k, :, cols])
        qv[:, cols] = value.astype(BF)

    gn.forward()
    loads[4].wait()
    loads[5].wait()
    loads[6].wait()

    def project(k):
        kv[k] = mm(N[k], wkv[...]).astype(BF)
        vv[k] = mm(N[k], wvv[...]).astype(BF)

    @pl.loop(0, 3)
    def _(s):
        project((me.z + (s + 3)) % 4 * 2 + me.c)

    gc.far()
    gn.near_pairs()

    @pl.loop(0, 3)
    def _(s):
        project((me.z + (s + 3)) % 4 * 2 + 1 - me.c)

    gc.pairs()
    gn.far()

    @pl.loop(0, 2)
    def _(m):
        cols = pl.ds(pl.multiple_of(m * 256, 256), 256)
        value = mm_nt(C[0], wov[cols, 0:512])
        for k in range(1, 8):
            value = value + mm_nt(C[k], wov[cols, k * 512:(k + 1) * 512])
        gav[:, cols] = value.astype(BF)

    project(me.tf)
    gn.last_pair()
    project((me.z + 2) % 4 * 2 + 1 - me.c)

    @pl.loop(0, 6, unroll=2)
    def _(s):
        rows = pl.ds(pl.multiple_of(s * 64, 64), 64)
        keys = pl.ds(pl.multiple_of(s * 32, 32), 32)
        attend(qv, gav, kv, vv, attv, gqv, gkv, gvv, rows, keys)

    @pl.loop(1, 16)
    def _(n):
        request(n, d).wait_send()
        fetch(n, d).wait_send()

    right_x = ((me.x + 1) % 4 * 4 + me.y, t)
    left_x = ((me.x + 3) % 4 * 4 + me.y, t)
    right_y = (me.x * 4 + (me.y + 1) % 4, t)
    left_y = (me.x * 4 + (me.y + 3) % 4, t)
    right_z, left_z = (d, me.tr), (d, me.tl)
    along = {"x": (me.x, right_x, left_x), "y": (me.y, right_y, left_y), "z": (me.z, right_z, left_z)}

    def ring(n, group, f1, f2, axis):
        return Ring(group, f1, f2, ss.at[n], sr.at[n], *along[axis])

    def pair(n, buf, f1, f2, f3, f4, first, second):
        mine = along[first][0]
        one = ring(n, lambda g, h: buf.at[g, h], f1, f2, first)
        two = ring(n + 1, lambda g, h: buf.at[mine, g // 2, (g % 2) * 2 + h], f3, f4, second)
        return one, two

    rq, rq2 = pair(0, Bq, q1, q2, q3, q4, "x", "y")
    ro, ro2 = pair(2, Bo, o1, o2, o3, o4, "y", "x")
    ra, ra2 = pair(4, Ba, a1, a2, a3, a4, "x", "y")
    rb, rb2 = pair(6, Bb, b1, b2, b3, b4, "y", "x")
    zo = ring(8, lambda g, h: H.at[g, pl.ds(h * 192, 192)], zo1, zo2, "z")
    zh = ring(9, lambda g, h: H.at[4 + g, pl.ds(h * 192, 192)], zh1, zh2, "z")
    zn = ring(10, lambda g, h: N.at[4 + g, pl.ds(h * 96, 96)], zn1, zn2, "z")

    attT[...] = attv[...].T
    gqT[...] = gqv[...].T

    kept = [
        pltpu.make_async_copy(a, b, keep.at[n])
        for n, (a, b) in enumerate(
            ((out_o, out_h), (hid_o, hid_h), (gq_o, gq_h), (go_o, go_h), (gk_o, gk_h), (gv_o, gv_h))
        )
    ]

    def weights(group_x, group_y):
        @pl.loop(0, 4)
        def _(s):
            dq = group_x * 4 + s
            do = s * 4 + group_y
            value = mm(gqT[...], H[dq // 2, :, pl.ds(pl.multiple_of((dq % 2) * 256, 256), 256)]).astype(BF)
            Bq[group_x, s // 2, (s % 2) * 2] = value[:256]
            Bq[group_x, s // 2, (s % 2) * 2 + 1] = value[256:]
            value = mm(attT[...], C[do // 2, :, pl.ds(pl.multiple_of((do % 2) * 256, 256), 256)]).astype(BF)
            Bo[group_y, s // 2, (s % 2) * 2] = value[:256]
            Bo[group_y, s // 2, (s % 2) * 2 + 1] = value[256:]

    weights(rq.r2, ro.r2)
    rq.first()
    ro.first()
    weights(rq.r1, ro.r1)
    weights(rq.l1, ro.l1)
    rq.second()
    ro.second()
    weights(rq.pos, ro.pos)
    for low, B in ((0, Ba), (256, Bb)):

        @pl.loop(0, 7)
        def _(m):
            cols = pl.ds(pl.multiple_of(m * 128, 128), 128)
            left = N[:, :, cols].reshape(1536, 128)
            GK[cols, :] = mm_tn(left, gkv[:, :, low:low + 256].reshape(1536, 256))
            GV[cols, :] = mm_tn(left, gvv[:, :, low:low + 256].reshape(1536, 256))

        @pl.loop(0, 16)
        def _(dd):
            rows = pl.ds(pl.multiple_of(dd * 56, 8), 56)
            value = jnp.concatenate([GK[rows, :], GV[rows, :]], axis=0).astype(BF)
            one, two = (dd // 4, dd % 4) if low == 0 else (dd % 4, dd // 4)
            B[one, two // 2, (two % 2) * 2] = value[:, :128]
            B[one, two // 2, (two % 2) * 2 + 1] = value[:, 128:]

    ra.first()
    rb.first()
    ra.second()
    rb.second()
    gn.sent()

    def terms(buf, base, core, product):
        @pl.loop(0, 4)
        def _(zz):
            buf[base + zz] = product(zz * 2 + core).astype(BF)

    def nbr_product(tt):
        return mm_nt(gkv[tt], wkv[...]) + mm_nt(gvv[tt], wvv[...])

    def out_product(tt):
        return mm(attv[...], wov[:, pl.ds(pl.multiple_of(tt * 512, 512), 512)])

    def hid_product(tt):
        return mm_nt(gqv[...], wqv[tt])

    def share(n, buf, base, P):
        return remote(buf.at[pl.ds(base, 4)], P, ps.at[n], pr.at[n], (d, me.partner))

    sn, so, sh = share(0, N, 0, Pn), share(1, C, 0, Po), share(2, C, 4, Ph)

    def merge(buf, base, P):
        @pl.loop(0, 4)
        def _(zz):
            add_into(buf.at[base + zz], P.at[zz])

    terms(N, 0, 1 - me.c, nbr_product)
    sn.start()
    terms(N, 4, me.c, nbr_product)
    sn.wait_recv()
    merge(N, 4, Pn)
    zn.first()
    zn.second()
    gh.sent()
    gc.sent()
    terms(C, 0, 1 - me.c, out_product)
    so.start()
    terms(H, 0, me.c, out_product)
    so.wait_recv()
    merge(H, 0, Po)
    zo.first()
    zo.second()
    rq.middle()
    ro.middle()
    zn.middle()
    terms(C, 4, 1 - me.c, hid_product)
    sh.start()
    terms(H, 4, me.c, hid_product)
    sh.wait_recv()
    merge(H, 4, Ph)
    zh.first()
    zh.second()
    zn.arrive()
    for h in range(2):
        value = zn.total(h).astype(BF)
        for k in range(6):
            encv[32 + h * 6 + k] = value[k * 16:(k + 1) * 16]
    encv[44] = jnp.zeros((16, 896), BF)
    def give(n, dst):
        return remote(encv.at[pl.ds(me.peer(n) * 2, 2)], ret.at[dst], bs.at[n], br.at[n], (me.peer(n), t))

    def choose(o, p):
        where = jnp.int32(12)
        for k in range(12):
            where = jnp.where(slots[k][0] * 2 + slots[k][1] == o * 2 + p, jnp.int32(k), where)
        return where

    @pl.loop(1, 16)
    def _(n):
        o = me.peer(n)
        for p in range(2):
            encv[o * 2 + p] = encv[32 + choose(o, p)]
        give(n, d).start()

    for p in range(2):
        ret[d, p] = encv[32 + choose(d, p)]
    zo.middle()
    zh.middle()
    rq.arrive()
    rq.sum_in_place()
    rq2.first()
    rq2.second()
    ro.arrive()
    ro.sum_in_place()
    ro2.first()
    ro2.second()
    ra.middle()
    rb.middle()
    rq2.middle()
    ro2.middle()
    ra.arrive()
    ra.sum_in_place()
    ra2.first()
    ra2.second()
    rb.arrive()
    rb.sum_in_place()
    rb2.first()
    rb2.second()
    rq2.arrive()
    for h in range(2):
        gq_o[:, h * 256:(h + 1) * 256] = rq2.total(h).T
    kept[2].start()
    ro2.arrive()
    for h in range(2):
        go_o[h * 256:(h + 1) * 256, :] = ro2.total(h)
    kept[3].start()
    ra2.middle()
    rb2.middle()
    zo.arrive()
    for h in range(2):
        out_o[h * 192:(h + 1) * 192, :] = zo.total(h).astype(BF)
    kept[0].start()
    zh.arrive()
    for h in range(2):
        hid_o[h * 192:(h + 1) * 192, :] = zh.total(h).astype(BF)
    kept[1].start()

    @pl.loop(1, 16)
    def _(n):
        give(n, me.source(n)).wait_recv()

    back = pltpu.make_async_copy(ret, ret_o, load.at[8])
    back.start()
    ra2.arrive()
    rb2.arrive()
    for h in range(2):
        for base, one in ((0, ra2), (256, rb2)):
            value = one.total(h)
            low = base + h * 128
            gk_o[:, low:low + 128] = value[:56]
            gv_o[:, low:low + 128] = value[56:]
    kept[4].start()
    kept[5].start()
    for one in (rq, ro, ra, rb, rq2, ro2, ra2, rb2, zo, zh, zn):
        one.sent()
    back.wait()
    for one in kept:
        one.wait()
    for one in (sn, so, sh):
        one.wait_send()

    @pl.loop(1, 16)
    def _(n):
        give(n, d).wait_send()


def layer_call(nbr_shard, nbr_row, hidden_in, cotangent, encodings, wq, wo, wk, wv):
    S = jax.ShapeDtypeStruct
    V = pltpu.VMEM
    tok, nbr, wide = V((384, 512), BF), V((8, 192, 512), BF), V((512, 384), BF)
    sizes = ((256, 256), (256, 256), (112, 128), (112, 128))
    big = [V((4, 2, 4, r, w), BF) for r, w in sizes]
    first, second, rings = [], [], []
    for r, w in sizes:
        first += [V((2, 4, r, w), BF), V((2, 2, 4, r, w), BF)]
        second += [V((2, r, w), BF), V((2, 2, r, w), BF)]
    for r, w in ((192, 512), (192, 512), (96, 896)):
        rings += [V((2, r, w), BF), V((2, 2, r, w), BF)]
    return pl.pallas_call(
        layer_kernel,
        name="layer",
        out_shape=(
            S((32,), jnp.int32), S((384, 512), BF), S((384, 512), BF), S((16, 2, 16, 896), BF),
            S((256, 512), F32), S((56, 512), F32), S((56, 512), F32), S((512, 256), F32),
        ),
        in_specs=[SM, SM] + [ANY] * 7,
        out_specs=(SM,) + (ANY,) * 7,
        scratch_shapes=[
            tok, tok, V((256, 512), F32), V((56, 512), F32), V((56, 512), F32), V((512, 256), F32),
            tok, tok, nbr, nbr,
            V((8, 384, 512), BF), V((8, 384, 512), BF), V((8, 192, 896), BF),
            V((64, 16, 896), BF), V((16, 2, 16, 896), BF), V((16, 2, 16, 896), BF),
            V((8, 128), jnp.int32), V((16, 8, 128), jnp.int32), pltpu.SMEM((16, 8, 128), jnp.int32),
            V((8, 512, 512), BF), V((512, 4096), BF), V((896, 512), BF), V((896, 512), BF),
            tok, tok, nbr, nbr, wide, wide, V((896, 256), F32), V((896, 256), F32),
        ]
        + big + first + second
        + [V((4, 384, 512), BF), V((4, 384, 512), BF), V((4, 192, 896), BF)]
        + rings
        + [
            V((16, 2, 16, 896), BF),
            DMA((9,)), DMA((3, 8)), DMA((3, 8)), DMA((16,)), DMA((16,)), DMA((16,)), DMA((16,)),
            DMA((3,)), DMA((3,)), DMA((11, 6)), DMA((11, 6)), DMA((16,)), DMA((16,)), DMA((6,)),
        ],
        compiler_params=pltpu.CompilerParams(
            collective_id=1, has_side_effects=True, vmem_limit_bytes=64 * 2**20 - 2**17
        ),
    )(nbr_shard, nbr_row, hidden_in, cotangent, encodings, wq, wo, wk, wv)


def finish_kernel(want_s, ret, *refs):
    kept, out_ref, given = refs[:6], refs[6], refs[7:13]
    retv, held, encv, get, put = refs[13], refs[14:20], refs[20], refs[21], refs[22]
    arrive = pltpu.make_async_copy(ret, retv, get.at[6])
    arrive.start()
    ins = [pltpu.make_async_copy(a, b, get.at[n]) for n, (a, b) in enumerate(zip(kept, held))]
    outs = [pltpu.make_async_copy(a, b, put.at[n]) for n, (a, b) in enumerate(zip(held, given))]
    for one in ins:
        one.start()
    encv[...] = jnp.zeros_like(encv)
    arrive.wait()

    @pl.loop(0, 32, unroll=4)
    def _(s):
        row = want_s[s]
        encv[row] += retv[s // 2, s % 2].astype(F32)

    parts = [
        pltpu.make_async_copy(encv.at[pl.ds(n * 16, 16)], out_ref.at[pl.ds(n * 16, 16)], put.at[6 + n])
        for n in range(4)
    ]
    for one in parts:
        one.start()
    for one, two in zip(ins, outs):
        one.wait()
        two.start()
    for one in outs + parts:
        one.wait()


def finish_call(want, ret, kept):
    S = jax.ShapeDtypeStruct
    return pl.pallas_call(
        finish_kernel,
        name="finish",
        out_shape=(S((64, 16, 896), F32),) + tuple(S(a.shape, a.dtype) for a in kept),
        in_specs=[SM] + [ANY] * 7,
        out_specs=(ANY,) * 7,
        scratch_shapes=[pltpu.VMEM((16, 2, 16, 896), BF)]
        + [pltpu.VMEM(a.shape, a.dtype) for a in kept]
        + [pltpu.VMEM((64, 16, 896), F32), DMA((7,)), DMA((10,))],
        compiler_params=pltpu.CompilerParams(vmem_limit_bytes=64 * 2**20 - 2**17),
    )(want, ret, *kept)


def shards(hidden_in, encodings, nbr_shard, nbr_row, w_query, w_key, w_value, w_output, cotangent):
    wq = w_query.reshape(8, 512, 512)
    owners, rows = nbr_shard.T, nbr_row.T
    want, out, hid, ret, sq, sk, sv, so = layer_call(
        owners, rows, hidden_in, cotangent, encodings, wq, w_output, w_key, w_value
    )
    enc, out, hid, sq, sk, sv, so = finish_call(want, ret, (out, hid, sq, sk, sv, so))
    return (out, hid, enc, sq, sk, sv, so)


def solution(mesh):
    return jax.shard_map(
        shards,
        mesh=mesh,
        in_specs=(
            P("dp", "tensor"),
            P("dp", "tensor", None),
            P("dp", None),
            P("dp", None),
            P(None, "tensor"),
            P(None, "tensor"),
            P(None, "tensor"),
            P("tensor", None),
            P("dp", "tensor"),
        ),
        out_specs=(
            P("dp", "tensor"),
            P("dp", "tensor"),
            P("dp", "tensor", None),
            P("dp", "tensor"),
            P("dp", "tensor"),
            P("dp", "tensor"),
            P("tensor", "dp"),
        ),
        check_vma=False,
    )
```

```python
import math

import jax
import jax.numpy as jnp
from jax import lax
from jax.experimental import pallas as pl
from jax.experimental.pallas import tpu as pltpu
from jax.sharding import PartitionSpec as P

HD = 128
SPAN = 64
NB = 128
K_NBR = 2
MESH = pl.DeviceIdType.MESH
BF = jnp.bfloat16
F32 = jnp.float32
ANY = pl.BlockSpec(memory_space=pl.ANY)
VM = pl.BlockSpec(memory_space=pltpu.VMEM)
SM = pl.BlockSpec(memory_space=pltpu.SMEM)
DMA = pltpu.SemaphoreType.DMA
NT = (((1,), (1,)), ((), ()))
TN = (((0,), (0,)), ((), ()))


def mm(a, b):
    return jnp.dot(a, b, preferred_element_type=F32)


def mm_nt(a, b):
    return lax.dot_general(a, b, NT, preferred_element_type=F32)


def mm_tn(a, b):
    return lax.dot_general(a, b, TN, preferred_element_type=F32)


class Place:
    def __init__(self):
        self.d = lax.axis_index("dp")
        self.t = lax.axis_index("tensor")
        self.x, self.y = self.d // 4, self.d % 4
        self.z, self.c = self.t // 2, self.t % 2
        self.partner = self.z * 2 + (1 - self.c)
        self.tr = ((self.z + 1) % 4) * 2 + self.c
        self.tl = ((self.z + 3) % 4) * 2 + self.c
        self.tf = ((self.z + 2) % 4) * 2 + self.c

    def peer(self, n):
        return (self.d + n) % 16

    def source(self, n):
        return (self.d + 16 - n) % 16

    def greet(self):
        barrier = pltpu.get_barrier_semaphore()
        for other in (self.partner, self.tr, self.tl):
            pl.semaphore_signal(barrier, inc=1, device_id=(self.d, other), device_id_type=MESH)

        @pl.loop(1, 16)
        def _(n):
            pl.semaphore_signal(barrier, inc=1, device_id=(self.peer(n), self.t), device_id_type=MESH)

        pl.semaphore_wait(barrier, 18)


def remote(src, dst, send, recv, dev):
    return pltpu.make_async_remote_copy(
        src_ref=src, dst_ref=dst, send_sem=send, recv_sem=recv, device_id=dev, device_id_type=MESH
    )


class Gather:
    def __init__(self, me, buf, half, send, recv):
        self.me, self.buf, self.half, self.send, self.recv = me, buf, half, send, recv

    def copy(self, n, t, dev, part=None):
        view = self.buf.at[t] if part is None else self.buf.at[t, pl.ds(part * self.half, self.half)]
        return remote(view, view, self.send.at[n], self.recv.at[n], (self.me.d, dev))

    def start(self):
        me = self.me
        self.copy(0, me.t, me.tr).start()
        self.copy(1, me.t, me.tl).start()
        self.copy(4, me.t, me.partner).start()

    def forward(self):
        me = self.me
        self.copy(0, me.tl, me.tr).wait_recv()
        self.copy(2, me.tl, me.tr, 0).start()
        self.copy(5, me.tl, me.partner).start()
        self.copy(1, me.tr, me.tl).wait_recv()
        self.copy(3, me.tr, me.tl, 1).start()
        self.copy(6, me.tr, me.partner).start()

    def far(self):
        me = self.me
        self.copy(2, me.tf, me.tr, 0).wait_recv()
        self.copy(3, me.tf, me.tl, 1).wait_recv()
        self.copy(7, me.tf, me.partner).start()

    def other(self, t):
        return t + 1 - 2 * self.me.c

    def near_pairs(self):
        me = self.me
        for n, t in ((4, me.t), (5, me.tl), (6, me.tr)):
            self.copy(n, self.other(t), me.partner).wait_recv()

    def last_pair(self):
        self.copy(7, self.other(self.me.tf), self.me.partner).wait_recv()

    def pairs(self):
        self.near_pairs()
        self.last_pair()

    def sent(self):
        me = self.me
        self.copy(0, me.t, me.tr).wait_send()
        self.copy(1, me.t, me.tl).wait_send()
        self.copy(2, me.tl, me.tr, 0).wait_send()
        self.copy(3, me.tr, me.tl, 1).wait_send()
        for n, t in ((4, me.t), (5, me.tl), (6, me.tr), (7, me.tf)):
            self.copy(n, t, me.partner).wait_send()


def attend(q_ref, ga_ref, k_ref, v_ref, att_ref, gq_ref, gk_ref, gv_ref, rows, keys):
    scale = 1.0 / math.sqrt(HD)
    heads = [slice(h * HD, (h + 1) * HD) for h in range(4)]
    q, ga = [q_ref[rows, c] for c in heads], [ga_ref[rows, c] for c in heads]
    k = [k_ref[:, keys, c].reshape(256, HD) for c in heads]
    v = [v_ref[:, keys, c].reshape(256, HD) for c in heads]
    s = [mm_nt(a, b) * scale for a, b in zip(q, k)]
    gp = [mm_nt(a, b) for a, b in zip(ga, v)]
    e = [jnp.exp(a - jnp.max(a, axis=-1, keepdims=True)) for a in s]
    p = [a * (1.0 / jnp.sum(a, axis=-1, keepdims=True)) for a in e]
    pb = [a.astype(BF) for a in p]
    inner = [jnp.sum(a * b, axis=-1, keepdims=True) for a, b in zip(gp, p)]
    gs = [(a * (b - c) * scale).astype(BF) for a, b, c in zip(p, gp, inner)]
    for n, c in enumerate(heads):
        att_ref[rows, c] = mm(pb[n], v[n]).astype(BF)
        gq_ref[rows, c] = mm(gs[n], k[n]).astype(BF)
    for n, c in enumerate(heads):
        gv_ref[:, keys, c] = mm_tn(pb[n], ga[n]).astype(BF).reshape(8, 32, HD)
        gk_ref[:, keys, c] = mm_tn(gs[n], q[n]).astype(BF).reshape(8, 32, HD)


class Ring:
    def __init__(self, group, f1, f2, send, recv, pos, right, left):
        self.group, self.f1, self.f2 = group, f1, f2
        self.pos = pos
        self.r1, self.r2, self.l1 = (pos + 1) % 4, (pos + 2) % 4, (pos + 3) % 4

        def cp(n, src, dst, dev):
            return remote(src, dst, send.at[n], recv.at[n], dev)

        self.s = [
            cp(0, group(self.r2, 0), f1.at[0], right),
            cp(1, group(self.r2, 1), f1.at[1], left),
            cp(2, group(self.r1, 1), f2.at[0, 1], right),
            cp(3, group(self.l1, 0), f2.at[1, 0], left),
            cp(4, group(self.r1, 0), f2.at[0, 0], right),
            cp(5, group(self.l1, 1), f2.at[1, 1], left),
        ]

    def first(self):
        self.s[0].start()
        self.s[1].start()

    def second(self):
        self.s[2].start()
        self.s[3].start()

    def middle(self):
        self.s[0].wait_recv()
        add_into(self.group(self.r1, 0), self.f1.at[0])
        self.s[4].start()
        self.s[1].wait_recv()
        add_into(self.group(self.l1, 1), self.f1.at[1])
        self.s[5].start()

    def arrive(self):
        for n in range(2, 6):
            self.s[n].wait_recv()

    def sum_in_place(self):
        for h in range(2):
            add_into(self.group(self.pos, h), self.f2.at[0, h], self.f2.at[1, h])

    def total(self, h):
        return (
            self.group(self.pos, h)[...].astype(F32)
            + self.f2[0, h].astype(F32)
            + self.f2[1, h].astype(F32)
        )

    def sent(self):
        for n in range(6):
            self.s[n].wait_send()


def add_into(dst, *srcs):
    lead, rows = dst.shape[:-2], dst.shape[-2]
    step = 32 if rows % 32 == 0 else 16

    def part(*where):
        value = dst[where].astype(F32)
        for src in srcs:
            value = value + src[where].astype(F32)
        dst[where] = value.astype(BF)

    if lead:

        @pl.loop(0, lead[0])
        def _(q):
            @pl.loop(0, rows // step)
            def _(r):
                part(q, pl.ds(pl.multiple_of(r * step, step), step))
    else:

        @pl.loop(0, rows // step)
        def _(r):
            part(pl.ds(pl.multiple_of(r * step, step), step))


def layer_kernel(
    shard_s, row_s, hid, cot, enc, wq, wo, wk, wv,
    want_o, out_h, hid_h, ret_o, gq_h, gk_h, gv_h, go_h,
    out_o, hid_o, gq_o, gk_o, gv_o, go_o,
    qv, gav, kv, vv, H, C, N, encv, outg, arr, req, wanted, want_s, wqv, wov, wkv, wvv,
    attv, gqv, gkv, gvv, attT, gqT, GK, GV,
    Bq, Bo, Ba, Bb, q1, q2, o1, o2, a1, a2, b1, b2, q3, q4, o3, o4, a3, a4, b3, b4,
    Po, Ph, Pn, zo1, zo2, zh1, zh2, zn1, zn2, ret,
    load, zs, zr, rs, rr, fs, fr, ps, pr, ss, sr, bs, br, keep,
):
    me = Place()
    d, t = me.d, me.t
    loads = [
        pltpu.make_async_copy(hid, H.at[t], load.at[0]),
        pltpu.make_async_copy(cot, C.at[t], load.at[1]),
        pltpu.make_async_copy(enc, encv, load.at[2]),
        pltpu.make_async_copy(wq, wqv, load.at[3]),
        pltpu.make_async_copy(wo, wov, load.at[4]),
        pltpu.make_async_copy(wk, wkv, load.at[5]),
        pltpu.make_async_copy(wv, wvv, load.at[6]),
    ]
    for one in loads:
        one.start()
    owners, slots = [], []
    lane = lax.broadcasted_iota(jnp.int32, (8, 128), 1)
    table = jnp.full((8, 128), 0, jnp.int32)
    for k in range(12):
        owner = shard_s[k % 2, k // 2]
        position = jnp.int32(0)
        for other in owners:
            position = position + (other == owner).astype(jnp.int32)
        owners.append(owner)
        slots.append((owner, jnp.minimum(position, 1)))
        table = jnp.where(lane == owner * 2 + position, row_s[k % 2, k // 2], table)
    req[...] = table
    wanted[d] = table
    me.greet()

    def request(n, dst):
        return remote(req, wanted.at[dst], rs.at[n], rr.at[n], (me.peer(n), t))

    @pl.loop(1, 16)
    def _(n):
        request(n, d).start()

    gh = Gather(me, H, 192, zs.at[0], zr.at[0])
    gc = Gather(me, C, 192, zs.at[1], zr.at[1])
    gn = Gather(me, N, 96, zs.at[2], zr.at[2])
    loads[0].wait()
    gh.start()
    loads[1].wait()
    gc.start()
    loads[2].wait()

    @pl.loop(1, 16)
    def _(n):
        request(n, me.source(n)).wait_recv()

    to_s = pltpu.make_async_copy(wanted, want_s, load.at[7])
    to_s.start()
    to_s.wait()

    def fetch(n, dst):
        return remote(outg.at[me.peer(n)], arr.at[dst], fs.at[n], fr.at[n], (me.peer(n), t))

    @pl.loop(1, 16)
    def _(n):
        reader = me.peer(n)
        for p in range(2):
            outg[reader, p] = encv[want_s[reader, 0, d * 2 + p]]
        fetch(n, d).start()

    for p in range(2):
        arr[d, p] = encv[want_s[d, 0, d * 2 + p]]
    gh.forward()

    @pl.loop(1, 16)
    def _(n):
        fetch(n, me.source(n)).wait_recv()

    for k in range(12):
        owner, position = slots[k]
        N[t, k * 16:(k + 1) * 16, :] = arr[owner, position]
    gn.start()
    gc.forward()
    gh.far()
    for r in range(16):
        for p in range(2):
            want_o[r * 2 + p] = want_s[r, 0, d * 2 + p]
    loads[3].wait()
    gh.pairs()

    @pl.loop(0, 2)
    def _(m):
        cols = pl.ds(pl.multiple_of(m * 256, 256), 256)
        value = mm(H[0], wqv[0, :, cols])
        for k in range(1, 8):
            value = value + mm(H[k], wqv[k, :, cols])
        qv[:, cols] = value.astype(BF)

    gn.forward()
    loads[4].wait()
    loads[5].wait()
    loads[6].wait()

    def project(k):
        kv[k] = mm(N[k], wkv[...]).astype(BF)
        vv[k] = mm(N[k], wvv[...]).astype(BF)

    @pl.loop(0, 3)
    def _(s):
        project((me.z + (s + 3)) % 4 * 2 + me.c)

    gc.far()
    gn.near_pairs()

    @pl.loop(0, 3)
    def _(s):
        project((me.z + (s + 3)) % 4 * 2 + 1 - me.c)

    gc.pairs()
    gn.far()

    @pl.loop(0, 2)
    def _(m):
        cols = pl.ds(pl.multiple_of(m * 256, 256), 256)
        value = mm_nt(C[0], wov[cols, 0:512])
        for k in range(1, 8):
            value = value + mm_nt(C[k], wov[cols, k * 512:(k + 1) * 512])
        gav[:, cols] = value.astype(BF)

    project(me.tf)
    gn.last_pair()
    project((me.z + 2) % 4 * 2 + 1 - me.c)

    @pl.loop(0, 6, unroll=2)
    def _(s):
        rows = pl.ds(pl.multiple_of(s * 64, 64), 64)
        keys = pl.ds(pl.multiple_of(s * 32, 32), 32)
        attend(qv, gav, kv, vv, attv, gqv, gkv, gvv, rows, keys)

    @pl.loop(1, 16)
    def _(n):
        request(n, d).wait_send()
        fetch(n, d).wait_send()

    right_x = ((me.x + 1) % 4 * 4 + me.y, t)
    left_x = ((me.x + 3) % 4 * 4 + me.y, t)
    right_y = (me.x * 4 + (me.y + 1) % 4, t)
    left_y = (me.x * 4 + (me.y + 3) % 4, t)
    right_z, left_z = (d, me.tr), (d, me.tl)
    along = {"x": (me.x, right_x, left_x), "y": (me.y, right_y, left_y), "z": (me.z, right_z, left_z)}

    def ring(n, group, f1, f2, axis):
        return Ring(group, f1, f2, ss.at[n], sr.at[n], *along[axis])

    def pair(n, buf, f1, f2, f3, f4, first, second):
        mine = along[first][0]
        one = ring(n, lambda g, h: buf.at[g, h], f1, f2, first)
        two = ring(n + 1, lambda g, h: buf.at[mine, g // 2, (g % 2) * 2 + h], f3, f4, second)
        return one, two

    rq, rq2 = pair(0, Bq, q1, q2, q3, q4, "x", "y")
    ro, ro2 = pair(2, Bo, o1, o2, o3, o4, "y", "x")
    ra, ra2 = pair(4, Ba, a1, a2, a3, a4, "x", "y")
    rb, rb2 = pair(6, Bb, b1, b2, b3, b4, "y", "x")
    zo = ring(8, lambda g, h: H.at[g, pl.ds(h * 192, 192)], zo1, zo2, "z")
    zh = ring(9, lambda g, h: H.at[4 + g, pl.ds(h * 192, 192)], zh1, zh2, "z")
    zn = ring(10, lambda g, h: N.at[4 + g, pl.ds(h * 96, 96)], zn1, zn2, "z")

    attT[...] = attv[...].T
    gqT[...] = gqv[...].T

    kept = [
        pltpu.make_async_copy(a, b, keep.at[n])
        for n, (a, b) in enumerate(
            ((out_o, out_h), (hid_o, hid_h), (gq_o, gq_h), (go_o, go_h), (gk_o, gk_h), (gv_o, gv_h))
        )
    ]

    def weights(group_x, group_y):
        @pl.loop(0, 4)
        def _(s):
            dq = group_x * 4 + s
            do = s * 4 + group_y
            value = mm(gqT[...], H[dq // 2, :, pl.ds(pl.multiple_of((dq % 2) * 256, 256), 256)]).astype(BF)
            Bq[group_x, s // 2, (s % 2) * 2] = value[:256]
            Bq[group_x, s // 2, (s % 2) * 2 + 1] = value[256:]
            value = mm(attT[...], C[do // 2, :, pl.ds(pl.multiple_of((do % 2) * 256, 256), 256)]).astype(BF)
            Bo[group_y, s // 2, (s % 2) * 2] = value[:256]
            Bo[group_y, s // 2, (s % 2) * 2 + 1] = value[256:]

    weights(rq.r2, ro.r2)
    rq.first()
    ro.first()
    weights(rq.r1, ro.r1)
    weights(rq.l1, ro.l1)
    rq.second()
    ro.second()
    weights(rq.pos, ro.pos)
    for low, B in ((0, Ba), (256, Bb)):

        @pl.loop(0, 7)
        def _(m):
            cols = pl.ds(pl.multiple_of(m * 128, 128), 128)
            left = N[:, :, cols].reshape(1536, 128)
            GK[cols, :] = mm_tn(left, gkv[:, :, low:low + 256].reshape(1536, 256))
            GV[cols, :] = mm_tn(left, gvv[:, :, low:low + 256].reshape(1536, 256))

        @pl.loop(0, 16)
        def _(dd):
            rows = pl.ds(pl.multiple_of(dd * 56, 8), 56)
            value = jnp.concatenate([GK[rows, :], GV[rows, :]], axis=0).astype(BF)
            one, two = (dd // 4, dd % 4) if low == 0 else (dd % 4, dd // 4)
            B[one, two // 2, (two % 2) * 2] = value[:, :128]
            B[one, two // 2, (two % 2) * 2 + 1] = value[:, 128:]

    ra.first()
    rb.first()
    ra.second()
    rb.second()
    gn.sent()

    def terms(buf, base, core, product):
        @pl.loop(0, 4)
        def _(zz):
            buf[base + zz] = product(zz * 2 + core).astype(BF)

    def nbr_product(tt):
        return mm_nt(gkv[tt], wkv[...]) + mm_nt(gvv[tt], wvv[...])

    def out_product(tt):
        return mm(attv[...], wov[:, pl.ds(pl.multiple_of(tt * 512, 512), 512)])

    def hid_product(tt):
        return mm_nt(gqv[...], wqv[tt])

    def share(n, buf, base, P):
        return remote(buf.at[pl.ds(base, 4)], P, ps.at[n], pr.at[n], (d, me.partner))

    sn, so, sh = share(0, N, 0, Pn), share(1, C, 0, Po), share(2, C, 4, Ph)

    def merge(buf, base, P):
        @pl.loop(0, 4)
        def _(zz):
            add_into(buf.at[base + zz], P.at[zz])

    terms(N, 0, 1 - me.c, nbr_product)
    sn.start()
    terms(N, 4, me.c, nbr_product)
    sn.wait_recv()
    merge(N, 4, Pn)
    zn.first()
    zn.second()
    gh.sent()
    gc.sent()
    terms(C, 0, 1 - me.c, out_product)
    so.start()
    terms(H, 0, me.c, out_product)
    so.wait_recv()
    merge(H, 0, Po)
    zo.first()
    zo.second()
    rq.middle()
    ro.middle()
    zn.middle()
    terms(C, 4, 1 - me.c, hid_product)
    sh.start()
    terms(H, 4, me.c, hid_product)
    sh.wait_recv()
    merge(H, 4, Ph)
    zh.first()
    zh.second()
    ra.middle()
    rb.middle()
    zn.arrive()
    for h in range(2):
        value = zn.total(h).astype(BF)
        for k in range(6):
            encv[32 + h * 6 + k] = value[k * 16:(k + 1) * 16]
    encv[44] = jnp.zeros((16, 896), BF)
    def give(n, dst):
        return remote(encv.at[pl.ds(me.peer(n) * 2, 2)], ret.at[dst], bs.at[n], br.at[n], (me.peer(n), t))

    def choose(o, p):
        where = jnp.int32(12)
        for k in range(12):
            where = jnp.where(slots[k][0] * 2 + slots[k][1] == o * 2 + p, jnp.int32(k), where)
        return where

    @pl.loop(1, 16)
    def _(n):
        o = me.peer(n)
        for p in range(2):
            encv[o * 2 + p] = encv[32 + choose(o, p)]
        give(n, d).start()

    for p in range(2):
        ret[d, p] = encv[32 + choose(d, p)]
    zo.middle()
    zh.middle()
    rq.arrive()
    rq.sum_in_place()
    rq2.first()
    rq2.second()
    ro.arrive()
    ro.sum_in_place()
    ro2.first()
    ro2.second()
    rq2.middle()
    ro2.middle()
    ra.arrive()
    ra.sum_in_place()
    ra2.first()
    ra2.second()
    rb.arrive()
    rb.sum_in_place()
    rb2.first()
    rb2.second()
    rq2.arrive()
    for h in range(2):
        gq_o[:, h * 256:(h + 1) * 256] = rq2.total(h).T
    kept[2].start()
    ro2.arrive()
    for h in range(2):
        go_o[h * 256:(h + 1) * 256, :] = ro2.total(h)
    kept[3].start()
    ra2.middle()
    rb2.middle()
    zo.arrive()
    for h in range(2):
        out_o[h * 192:(h + 1) * 192, :] = zo.total(h).astype(BF)
    kept[0].start()
    zh.arrive()
    for h in range(2):
        hid_o[h * 192:(h + 1) * 192, :] = zh.total(h).astype(BF)
    kept[1].start()

    @pl.loop(1, 16)
    def _(n):
        give(n, me.source(n)).wait_recv()

    back = pltpu.make_async_copy(ret, ret_o, load.at[8])
    back.start()
    ra2.arrive()
    rb2.arrive()
    for h in range(2):
        for base, one in ((0, ra2), (256, rb2)):
            value = one.total(h)
            low = base + h * 128
            gk_o[:, low:low + 128] = value[:56]
            gv_o[:, low:low + 128] = value[56:]
    kept[4].start()
    kept[5].start()
    for one in (rq, ro, ra, rb, rq2, ro2, ra2, rb2, zo, zh, zn):
        one.sent()
    back.wait()
    for one in kept:
        one.wait()
    for one in (sn, so, sh):
        one.wait_send()

    @pl.loop(1, 16)
    def _(n):
        give(n, d).wait_send()


def layer_call(nbr_shard, nbr_row, hidden_in, cotangent, encodings, wq, wo, wk, wv):
    S = jax.ShapeDtypeStruct
    V = pltpu.VMEM
    tok, nbr, wide = V((384, 512), BF), V((8, 192, 512), BF), V((512, 384), BF)
    sizes = ((256, 256), (256, 256), (112, 128), (112, 128))
    big = [V((4, 2, 4, r, w), BF) for r, w in sizes]
    first, second, rings = [], [], []
    for r, w in sizes:
        first += [V((2, 4, r, w), BF), V((2, 2, 4, r, w), BF)]
        second += [V((2, r, w), BF), V((2, 2, r, w), BF)]
    for r, w in ((192, 512), (192, 512), (96, 896)):
        rings += [V((2, r, w), BF), V((2, 2, r, w), BF)]
    return pl.pallas_call(
        layer_kernel,
        name="layer",
        out_shape=(
            S((32,), jnp.int32), S((384, 512), BF), S((384, 512), BF), S((16, 2, 16, 896), BF),
            S((256, 512), F32), S((56, 512), F32), S((56, 512), F32), S((512, 256), F32),
        ),
        in_specs=[SM, SM] + [ANY] * 7,
        out_specs=(SM,) + (ANY,) * 7,
        scratch_shapes=[
            tok, tok, V((256, 512), F32), V((56, 512), F32), V((56, 512), F32), V((512, 256), F32),
            tok, tok, nbr, nbr,
            V((8, 384, 512), BF), V((8, 384, 512), BF), V((8, 192, 896), BF),
            V((64, 16, 896), BF), V((16, 2, 16, 896), BF), V((16, 2, 16, 896), BF),
            V((8, 128), jnp.int32), V((16, 8, 128), jnp.int32), pltpu.SMEM((16, 8, 128), jnp.int32),
            V((8, 512, 512), BF), V((512, 4096), BF), V((896, 512), BF), V((896, 512), BF),
            tok, tok, nbr, nbr, wide, wide, V((896, 256), F32), V((896, 256), F32),
        ]
        + big + first + second
        + [V((4, 384, 512), BF), V((4, 384, 512), BF), V((4, 192, 896), BF)]
        + rings
        + [
            V((16, 2, 16, 896), BF),
            DMA((9,)), DMA((3, 8)), DMA((3, 8)), DMA((16,)), DMA((16,)), DMA((16,)), DMA((16,)),
            DMA((3,)), DMA((3,)), DMA((11, 6)), DMA((11, 6)), DMA((16,)), DMA((16,)), DMA((6,)),
        ],
        compiler_params=pltpu.CompilerParams(
            collective_id=1, has_side_effects=True, vmem_limit_bytes=64 * 2**20 - 2**17
        ),
    )(nbr_shard, nbr_row, hidden_in, cotangent, encodings, wq, wo, wk, wv)


def finish_kernel(want_s, ret, *refs):
    kept, out_ref, given = refs[:6], refs[6], refs[7:13]
    retv, held, encv, get, put = refs[13], refs[14:20], refs[20], refs[21], refs[22]
    arrive = pltpu.make_async_copy(ret, retv, get.at[6])
    arrive.start()
    ins = [pltpu.make_async_copy(a, b, get.at[n]) for n, (a, b) in enumerate(zip(kept, held))]
    outs = [pltpu.make_async_copy(a, b, put.at[n]) for n, (a, b) in enumerate(zip(held, given))]
    for one in ins:
        one.start()
    encv[...] = jnp.zeros_like(encv)
    arrive.wait()

    @pl.loop(0, 32, unroll=4)
    def _(s):
        row = want_s[s]
        encv[row] += retv[s // 2, s % 2].astype(F32)

    parts = [
        pltpu.make_async_copy(encv.at[pl.ds(n * 16, 16)], out_ref.at[pl.ds(n * 16, 16)], put.at[6 + n])
        for n in range(4)
    ]
    for one in parts:
        one.start()
    for one, two in zip(ins, outs):
        one.wait()
        two.start()
    for one in outs + parts:
        one.wait()


def finish_call(want, ret, kept):
    S = jax.ShapeDtypeStruct
    return pl.pallas_call(
        finish_kernel,
        name="finish",
        out_shape=(S((64, 16, 896), F32),) + tuple(S(a.shape, a.dtype) for a in kept),
        in_specs=[SM] + [ANY] * 7,
        out_specs=(ANY,) * 7,
        scratch_shapes=[pltpu.VMEM((16, 2, 16, 896), BF)]
        + [pltpu.VMEM(a.shape, a.dtype) for a in kept]
        + [pltpu.VMEM((64, 16, 896), F32), DMA((7,)), DMA((10,))],
        compiler_params=pltpu.CompilerParams(vmem_limit_bytes=64 * 2**20 - 2**17),
    )(want, ret, *kept)


def shards(hidden_in, encodings, nbr_shard, nbr_row, w_query, w_key, w_value, w_output, cotangent):
    wq = w_query.reshape(8, 512, 512)
    owners, rows = nbr_shard.T, nbr_row.T
    want, out, hid, ret, sq, sk, sv, so = layer_call(
        owners, rows, hidden_in, cotangent, encodings, wq, w_output, w_key, w_value
    )
    enc, out, hid, sq, sk, sv, so = finish_call(want, ret, (out, hid, sq, sk, sv, so))
    return (out, hid, enc, sq, sk, sv, so)


def solution(mesh):
    return jax.shard_map(
        shards,
        mesh=mesh,
        in_specs=(
            P("dp", "tensor"),
            P("dp", "tensor", None),
            P("dp", None),
            P("dp", None),
            P(None, "tensor"),
            P(None, "tensor"),
            P(None, "tensor"),
            P("tensor", None),
            P("dp", "tensor"),
        ),
        out_specs=(
            P("dp", "tensor"),
            P("dp", "tensor"),
            P("dp", "tensor", None),
            P("dp", "tensor"),
            P("dp", "tensor"),
            P("dp", "tensor"),
            P("tensor", "dp"),
        ),
        check_vma=False,
    )
```

```python
import math

import jax
import jax.numpy as jnp
from jax import lax
from jax.experimental import pallas as pl
from jax.experimental.pallas import tpu as pltpu
from jax.sharding import PartitionSpec as P

HD = 128
SPAN = 64
NB = 128
K_NBR = 2
MESH = pl.DeviceIdType.MESH
BF = jnp.bfloat16
F32 = jnp.float32
ANY = pl.BlockSpec(memory_space=pl.ANY)
VM = pl.BlockSpec(memory_space=pltpu.VMEM)
SM = pl.BlockSpec(memory_space=pltpu.SMEM)
DMA = pltpu.SemaphoreType.DMA
NT = (((1,), (1,)), ((), ()))
TN = (((0,), (0,)), ((), ()))


def mm(a, b):
    return jnp.dot(a, b, preferred_element_type=F32)


def mm_nt(a, b):
    return lax.dot_general(a, b, NT, preferred_element_type=F32)


def mm_tn(a, b):
    return lax.dot_general(a, b, TN, preferred_element_type=F32)


class Place:
    def __init__(self):
        self.d = lax.axis_index("dp")
        self.t = lax.axis_index("tensor")
        self.x, self.y = self.d // 4, self.d % 4
        self.z, self.c = self.t // 2, self.t % 2
        self.partner = self.z * 2 + (1 - self.c)
        self.tr = ((self.z + 1) % 4) * 2 + self.c
        self.tl = ((self.z + 3) % 4) * 2 + self.c
        self.tf = ((self.z + 2) % 4) * 2 + self.c

    def peer(self, n):
        return (self.d + n) % 16

    def source(self, n):
        return (self.d + 16 - n) % 16

    def greet(self):
        barrier = pltpu.get_barrier_semaphore()
        for other in (self.partner, self.tr, self.tl):
            pl.semaphore_signal(barrier, inc=1, device_id=(self.d, other), device_id_type=MESH)

        @pl.loop(1, 16)
        def _(n):
            pl.semaphore_signal(barrier, inc=1, device_id=(self.peer(n), self.t), device_id_type=MESH)

        pl.semaphore_wait(barrier, 18)


def remote(src, dst, send, recv, dev):
    return pltpu.make_async_remote_copy(
        src_ref=src, dst_ref=dst, send_sem=send, recv_sem=recv, device_id=dev, device_id_type=MESH
    )


class Gather:
    def __init__(self, me, buf, half, send, recv):
        self.me, self.buf, self.half, self.send, self.recv = me, buf, half, send, recv

    def copy(self, n, t, dev, part=None):
        view = self.buf.at[t] if part is None else self.buf.at[t, pl.ds(part * self.half, self.half)]
        return remote(view, view, self.send.at[n], self.recv.at[n], (self.me.d, dev))

    def start(self):
        me = self.me
        self.copy(0, me.t, me.tr).start()
        self.copy(1, me.t, me.tl).start()
        self.copy(4, me.t, me.partner).start()

    def forward(self):
        me = self.me
        self.copy(0, me.tl, me.tr).wait_recv()
        self.copy(2, me.tl, me.tr, 0).start()
        self.copy(5, me.tl, me.partner).start()
        self.copy(1, me.tr, me.tl).wait_recv()
        self.copy(3, me.tr, me.tl, 1).start()
        self.copy(6, me.tr, me.partner).start()

    def far(self):
        me = self.me
        self.copy(2, me.tf, me.tr, 0).wait_recv()
        self.copy(3, me.tf, me.tl, 1).wait_recv()
        self.copy(7, me.tf, me.partner).start()

    def other(self, t):
        return t + 1 - 2 * self.me.c

    def near_pairs(self):
        me = self.me
        for n, t in ((4, me.t), (5, me.tl), (6, me.tr)):
            self.copy(n, self.other(t), me.partner).wait_recv()

    def last_pair(self):
        self.copy(7, self.other(self.me.tf), self.me.partner).wait_recv()

    def pairs(self):
        self.near_pairs()
        self.last_pair()

    def sent(self):
        me = self.me
        self.copy(0, me.t, me.tr).wait_send()
        self.copy(1, me.t, me.tl).wait_send()
        self.copy(2, me.tl, me.tr, 0).wait_send()
        self.copy(3, me.tr, me.tl, 1).wait_send()
        for n, t in ((4, me.t), (5, me.tl), (6, me.tr), (7, me.tf)):
            self.copy(n, t, me.partner).wait_send()


def attend(q_ref, ga_ref, k_ref, v_ref, att_ref, gq_ref, gk_ref, gv_ref, rows, keys):
    scale = 1.0 / math.sqrt(HD)
    heads = [slice(h * HD, (h + 1) * HD) for h in range(4)]
    q, ga = [q_ref[rows, c] for c in heads], [ga_ref[rows, c] for c in heads]
    k = [k_ref[:, keys, c].reshape(256, HD) for c in heads]
    v = [v_ref[:, keys, c].reshape(256, HD) for c in heads]
    s = [mm_nt(a, b) * scale for a, b in zip(q, k)]
    gp = [mm_nt(a, b) for a, b in zip(ga, v)]
    e = [jnp.exp(a - jnp.max(a, axis=-1, keepdims=True)) for a in s]
    p = [a * (1.0 / jnp.sum(a, axis=-1, keepdims=True)) for a in e]
    pb = [a.astype(BF) for a in p]
    inner = [jnp.sum(a * b, axis=-1, keepdims=True) for a, b in zip(gp, p)]
    gs = [(a * (b - c) * scale).astype(BF) for a, b, c in zip(p, gp, inner)]
    for n, c in enumerate(heads):
        att_ref[rows, c] = mm(pb[n], v[n]).astype(BF)
        gq_ref[rows, c] = mm(gs[n], k[n]).astype(BF)
    for n, c in enumerate(heads):
        gv_ref[:, keys, c] = mm_tn(pb[n], ga[n]).astype(BF).reshape(8, 32, HD)
        gk_ref[:, keys, c] = mm_tn(gs[n], q[n]).astype(BF).reshape(8, 32, HD)


class Ring:
    def __init__(self, group, f1, f2, send, recv, pos, right, left):
        self.group, self.f1, self.f2 = group, f1, f2
        self.pos = pos
        self.r1, self.r2, self.l1 = (pos + 1) % 4, (pos + 2) % 4, (pos + 3) % 4

        def cp(n, src, dst, dev):
            return remote(src, dst, send.at[n], recv.at[n], dev)

        self.s = [
            cp(0, group(self.r2, 0), f1.at[0], right),
            cp(1, group(self.r2, 1), f1.at[1], left),
            cp(2, group(self.r1, 1), f2.at[0, 1], right),
            cp(3, group(self.l1, 0), f2.at[1, 0], left),
            cp(4, group(self.r1, 0), f2.at[0, 0], right),
            cp(5, group(self.l1, 1), f2.at[1, 1], left),
        ]

    def first(self):
        self.s[0].start()
        self.s[1].start()

    def second(self):
        self.s[2].start()
        self.s[3].start()

    def middle(self):
        self.s[0].wait_recv()
        add_into(self.group(self.r1, 0), self.f1.at[0])
        self.s[4].start()
        self.s[1].wait_recv()
        add_into(self.group(self.l1, 1), self.f1.at[1])
        self.s[5].start()

    def arrive(self):
        for n in range(2, 6):
            self.s[n].wait_recv()

    def sum_in_place(self):
        for h in range(2):
            add_into(self.group(self.pos, h), self.f2.at[0, h], self.f2.at[1, h])

    def total(self, h):
        return (
            self.group(self.pos, h)[...].astype(F32)
            + self.f2[0, h].astype(F32)
            + self.f2[1, h].astype(F32)
        )

    def sent(self):
        for n in range(6):
            self.s[n].wait_send()


def add_into(dst, *srcs):
    lead, rows = dst.shape[:-2], dst.shape[-2]
    step = 32 if rows % 32 == 0 else 16

    def part(*where):
        value = dst[where].astype(F32)
        for src in srcs:
            value = value + src[where].astype(F32)
        dst[where] = value.astype(BF)

    if lead:

        @pl.loop(0, lead[0])
        def _(q):
            @pl.loop(0, rows // step)
            def _(r):
                part(q, pl.ds(pl.multiple_of(r * step, step), step))
    else:

        @pl.loop(0, rows // step)
        def _(r):
            part(pl.ds(pl.multiple_of(r * step, step), step))


def layer_kernel(
    shard_s, row_s, hid, cot, enc, wq, wo, wk, wv,
    want_o, out_h, hid_h, ret_o, gq_h, gk_h, gv_h, go_h,
    out_o, hid_o, gq_o, gk_o, gv_o, go_o,
    qv, gav, kv, vv, H, C, N, encv, outg, arr, req, wanted, want_s, wqv, wov, wkv, wvv,
    attv, gqv, gkv, gvv, attT, gqT, GK, GV,
    Bq, Bo, Ba, Bb, q1, q2, o1, o2, a1, a2, b1, b2, q3, q4, o3, o4, a3, a4, b3, b4,
    Po, Ph, Pn, zo1, zo2, zh1, zh2, zn1, zn2, ret,
    load, zs, zr, rs, rr, fs, fr, ps, pr, ss, sr, bs, br, keep,
):
    me = Place()
    d, t = me.d, me.t
    loads = [
        pltpu.make_async_copy(hid, H.at[t], load.at[0]),
        pltpu.make_async_copy(cot, C.at[t], load.at[1]),
        pltpu.make_async_copy(enc, encv, load.at[2]),
        pltpu.make_async_copy(wq, wqv, load.at[3]),
        pltpu.make_async_copy(wo, wov, load.at[4]),
        pltpu.make_async_copy(wk, wkv, load.at[5]),
        pltpu.make_async_copy(wv, wvv, load.at[6]),
    ]
    for one in loads:
        one.start()
    owners, slots = [], []
    lane = lax.broadcasted_iota(jnp.int32, (8, 128), 1)
    table = jnp.full((8, 128), 0, jnp.int32)
    for k in range(12):
        owner = shard_s[k % 2, k // 2]
        position = jnp.int32(0)
        for other in owners:
            position = position + (other == owner).astype(jnp.int32)
        owners.append(owner)
        slots.append((owner, jnp.minimum(position, 1)))
        table = jnp.where(lane == owner * 2 + position, row_s[k % 2, k // 2], table)
    req[...] = table
    wanted[d] = table
    me.greet()

    def request(n, dst):
        return remote(req, wanted.at[dst], rs.at[n], rr.at[n], (me.peer(n), t))

    @pl.loop(1, 16)
    def _(n):
        request(n, d).start()

    gh = Gather(me, H, 192, zs.at[0], zr.at[0])
    gc = Gather(me, C, 192, zs.at[1], zr.at[1])
    gn = Gather(me, N, 96, zs.at[2], zr.at[2])
    loads[0].wait()
    gh.start()
    loads[1].wait()
    gc.start()
    loads[2].wait()

    @pl.loop(1, 16)
    def _(n):
        request(n, me.source(n)).wait_recv()

    to_s = pltpu.make_async_copy(wanted, want_s, load.at[7])
    to_s.start()
    to_s.wait()

    def fetch(n, dst):
        return remote(outg.at[me.peer(n)], arr.at[dst], fs.at[n], fr.at[n], (me.peer(n), t))

    @pl.loop(1, 16)
    def _(n):
        reader = me.peer(n)
        for p in range(2):
            outg[reader, p] = encv[want_s[reader, 0, d * 2 + p]]
        fetch(n, d).start()

    for p in range(2):
        arr[d, p] = encv[want_s[d, 0, d * 2 + p]]
    gh.forward()

    @pl.loop(1, 16)
    def _(n):
        fetch(n, me.source(n)).wait_recv()

    for k in range(12):
        owner, position = slots[k]
        N[t, k * 16:(k + 1) * 16, :] = arr[owner, position]
    gn.start()
    gc.forward()
    gh.far()
    for r in range(16):
        for p in range(2):
            want_o[r * 2 + p] = want_s[r, 0, d * 2 + p]
    loads[3].wait()
    gh.pairs()

    @pl.loop(0, 2)
    def _(m):
        cols = pl.ds(pl.multiple_of(m * 256, 256), 256)
        value = mm(H[0], wqv[0, :, cols])
        for k in range(1, 8):
            value = value + mm(H[k], wqv[k, :, cols])
        qv[:, cols] = value.astype(BF)

    gn.forward()
    loads[4].wait()
    loads[5].wait()
    loads[6].wait()

    def project(k):
        kv[k] = mm(N[k], wkv[...]).astype(BF)
        vv[k] = mm(N[k], wvv[...]).astype(BF)

    @pl.loop(0, 3)
    def _(s):
        project((me.z + (s + 3)) % 4 * 2 + me.c)

    gc.far()
    gn.near_pairs()

    @pl.loop(0, 3)
    def _(s):
        project((me.z + (s + 3)) % 4 * 2 + 1 - me.c)

    gc.pairs()
    gn.far()

    @pl.loop(0, 2)
    def _(m):
        cols = pl.ds(pl.multiple_of(m * 256, 256), 256)
        value = mm_nt(C[0], wov[cols, 0:512])
        for k in range(1, 8):
            value = value + mm_nt(C[k], wov[cols, k * 512:(k + 1) * 512])
        gav[:, cols] = value.astype(BF)

    project(me.tf)
    gn.last_pair()
    project((me.z + 2) % 4 * 2 + 1 - me.c)

    @pl.loop(0, 6, unroll=2)
    def _(s):
        rows = pl.ds(pl.multiple_of(s * 64, 64), 64)
        keys = pl.ds(pl.multiple_of(s * 32, 32), 32)
        attend(qv, gav, kv, vv, attv, gqv, gkv, gvv, rows, keys)

    @pl.loop(1, 16)
    def _(n):
        request(n, d).wait_send()
        fetch(n, d).wait_send()

    right_x = ((me.x + 1) % 4 * 4 + me.y, t)
    left_x = ((me.x + 3) % 4 * 4 + me.y, t)
    right_y = (me.x * 4 + (me.y + 1) % 4, t)
    left_y = (me.x * 4 + (me.y + 3) % 4, t)
    right_z, left_z = (d, me.tr), (d, me.tl)
    along = {"x": (me.x, right_x, left_x), "y": (me.y, right_y, left_y), "z": (me.z, right_z, left_z)}

    def ring(n, group, f1, f2, axis):
        return Ring(group, f1, f2, ss.at[n], sr.at[n], *along[axis])

    def pair(n, buf, f1, f2, f3, f4, first, second):
        mine = along[first][0]
        one = ring(n, lambda g, h: buf.at[g, h], f1, f2, first)
        two = ring(n + 1, lambda g, h: buf.at[mine, g // 2, (g % 2) * 2 + h], f3, f4, second)
        return one, two

    rq, rq2 = pair(0, Bq, q1, q2, q3, q4, "x", "y")
    ro, ro2 = pair(2, Bo, o1, o2, o3, o4, "y", "x")
    ra, ra2 = pair(4, Ba, a1, a2, a3, a4, "x", "y")
    rb, rb2 = pair(6, Bb, b1, b2, b3, b4, "y", "x")
    zo = ring(8, lambda g, h: H.at[g, pl.ds(h * 192, 192)], zo1, zo2, "z")
    zh = ring(9, lambda g, h: H.at[4 + g, pl.ds(h * 192, 192)], zh1, zh2, "z")
    zn = ring(10, lambda g, h: N.at[4 + g, pl.ds(h * 96, 96)], zn1, zn2, "z")

    attT[...] = attv[...].T
    gqT[...] = gqv[...].T

    kept = [
        pltpu.make_async_copy(a, b, keep.at[n])
        for n, (a, b) in enumerate(
            ((out_o, out_h), (hid_o, hid_h), (gq_o, gq_h), (go_o, go_h), (gk_o, gk_h), (gv_o, gv_h))
        )
    ]

    def weights(group_x, group_y):
        @pl.loop(0, 4)
        def _(s):
            dq = group_x * 4 + s
            do = s * 4 + group_y
            value = mm(gqT[...], H[dq // 2, :, pl.ds(pl.multiple_of((dq % 2) * 256, 256), 256)]).astype(BF)
            Bq[group_x, s // 2, (s % 2) * 2] = value[:256]
            Bq[group_x, s // 2, (s % 2) * 2 + 1] = value[256:]
            value = mm(attT[...], C[do // 2, :, pl.ds(pl.multiple_of((do % 2) * 256, 256), 256)]).astype(BF)
            Bo[group_y, s // 2, (s % 2) * 2] = value[:256]
            Bo[group_y, s // 2, (s % 2) * 2 + 1] = value[256:]

    weights(rq.r2, ro.r2)
    rq.first()
    ro.first()
    weights(rq.r1, ro.r1)
    weights(rq.l1, ro.l1)
    rq.second()
    ro.second()
    weights(rq.pos, ro.pos)
    for low, B in ((0, Ba), (256, Bb)):

        @pl.loop(0, 7)
        def _(m):
            cols = pl.ds(pl.multiple_of(m * 128, 128), 128)
            left = N[:, :, cols].reshape(1536, 128)
            GK[cols, :] = mm_tn(left, gkv[:, :, low:low + 256].reshape(1536, 256))
            GV[cols, :] = mm_tn(left, gvv[:, :, low:low + 256].reshape(1536, 256))

        @pl.loop(0, 16)
        def _(dd):
            rows = pl.ds(pl.multiple_of(dd * 56, 8), 56)
            value = jnp.concatenate([GK[rows, :], GV[rows, :]], axis=0).astype(BF)
            one, two = (dd // 4, dd % 4) if low == 0 else (dd % 4, dd // 4)
            B[one, two // 2, (two % 2) * 2] = value[:, :128]
            B[one, two // 2, (two % 2) * 2 + 1] = value[:, 128:]

    ra.first()
    rb.first()
    ra.second()
    rb.second()
    gn.sent()

    def terms(buf, base, core, product):
        @pl.loop(0, 4)
        def _(zz):
            buf[base + zz] = product(zz * 2 + core).astype(BF)

    def nbr_product(tt):
        return mm_nt(gkv[tt], wkv[...]) + mm_nt(gvv[tt], wvv[...])

    def out_product(tt):
        return mm(attv[...], wov[:, pl.ds(pl.multiple_of(tt * 512, 512), 512)])

    def hid_product(tt):
        return mm_nt(gqv[...], wqv[tt])

    def share(n, buf, base, P):
        return remote(buf.at[pl.ds(base, 4)], P, ps.at[n], pr.at[n], (d, me.partner))

    sn, so, sh = share(0, N, 0, Pn), share(1, C, 0, Po), share(2, C, 4, Ph)

    def merge(buf, base, P):
        @pl.loop(0, 4)
        def _(zz):
            add_into(buf.at[base + zz], P.at[zz])

    terms(N, 0, 1 - me.c, nbr_product)
    sn.start()
    terms(N, 4, me.c, nbr_product)
    sn.wait_recv()
    merge(N, 4, Pn)
    zn.first()
    zn.second()
    gh.sent()
    gc.sent()
    terms(C, 0, 1 - me.c, out_product)
    so.start()
    terms(H, 0, me.c, out_product)
    so.wait_recv()
    merge(H, 0, Po)
    zo.first()
    zo.second()
    rq.middle()
    ro.middle()
    zn.middle()
    terms(C, 4, 1 - me.c, hid_product)
    sh.start()
    terms(H, 4, me.c, hid_product)
    sh.wait_recv()
    merge(H, 4, Ph)
    zh.first()
    zh.second()
    ra.middle()
    rb.middle()
    zn.arrive()
    for h in range(2):
        value = zn.total(h).astype(BF)
        for k in range(6):
            encv[32 + h * 6 + k] = value[k * 16:(k + 1) * 16]
    encv[44] = jnp.zeros((16, 896), BF)
    def give(n, dst):
        return remote(encv.at[pl.ds(me.peer(n) * 2, 2)], ret.at[dst], bs.at[n], br.at[n], (me.peer(n), t))

    def choose(o, p):
        where = jnp.int32(12)
        for k in range(12):
            where = jnp.where(slots[k][0] * 2 + slots[k][1] == o * 2 + p, jnp.int32(k), where)
        return where

    zo.middle()
    zh.middle()
    rq.arrive()
    rq.sum_in_place()
    rq2.first()
    rq2.second()
    @pl.loop(1, 16)
    def _(n):
        o = me.peer(n)
        for p in range(2):
            encv[o * 2 + p] = encv[32 + choose(o, p)]
        give(n, d).start()

    for p in range(2):
        ret[d, p] = encv[32 + choose(d, p)]
    ro.arrive()
    ro.sum_in_place()
    ro2.first()
    ro2.second()
    rq2.middle()
    ro2.middle()
    ra.arrive()
    ra.sum_in_place()
    ra2.first()
    ra2.second()
    rb.arrive()
    rb.sum_in_place()
    rb2.first()
    rb2.second()
    rq2.arrive()
    for h in range(2):
        gq_o[:, h * 256:(h + 1) * 256] = rq2.total(h).T
    kept[2].start()
    ro2.arrive()
    for h in range(2):
        go_o[h * 256:(h + 1) * 256, :] = ro2.total(h)
    kept[3].start()
    ra2.middle()
    rb2.middle()
    zo.arrive()
    for h in range(2):
        out_o[h * 192:(h + 1) * 192, :] = zo.total(h).astype(BF)
    kept[0].start()
    zh.arrive()
    for h in range(2):
        hid_o[h * 192:(h + 1) * 192, :] = zh.total(h).astype(BF)
    kept[1].start()

    @pl.loop(1, 16)
    def _(n):
        give(n, me.source(n)).wait_recv()

    back = pltpu.make_async_copy(ret, ret_o, load.at[8])
    back.start()
    ra2.arrive()
    rb2.arrive()
    for h in range(2):
        for base, one in ((0, ra2), (256, rb2)):
            value = one.total(h)
            low = base + h * 128
            gk_o[:, low:low + 128] = value[:56]
            gv_o[:, low:low + 128] = value[56:]
    kept[4].start()
    kept[5].start()
    for one in (rq, ro, ra, rb, rq2, ro2, ra2, rb2, zo, zh, zn):
        one.sent()
    back.wait()
    for one in kept:
        one.wait()
    for one in (sn, so, sh):
        one.wait_send()

    @pl.loop(1, 16)
    def _(n):
        give(n, d).wait_send()


def layer_call(nbr_shard, nbr_row, hidden_in, cotangent, encodings, wq, wo, wk, wv):
    S = jax.ShapeDtypeStruct
    V = pltpu.VMEM
    tok, nbr, wide = V((384, 512), BF), V((8, 192, 512), BF), V((512, 384), BF)
    sizes = ((256, 256), (256, 256), (112, 128), (112, 128))
    big = [V((4, 2, 4, r, w), BF) for r, w in sizes]
    first, second, rings = [], [], []
    for r, w in sizes:
        first += [V((2, 4, r, w), BF), V((2, 2, 4, r, w), BF)]
        second += [V((2, r, w), BF), V((2, 2, r, w), BF)]
    for r, w in ((192, 512), (192, 512), (96, 896)):
        rings += [V((2, r, w), BF), V((2, 2, r, w), BF)]
    return pl.pallas_call(
        layer_kernel,
        name="layer",
        out_shape=(
            S((32,), jnp.int32), S((384, 512), BF), S((384, 512), BF), S((16, 2, 16, 896), BF),
            S((256, 512), F32), S((56, 512), F32), S((56, 512), F32), S((512, 256), F32),
        ),
        in_specs=[SM, SM] + [ANY] * 7,
        out_specs=(SM,) + (ANY,) * 7,
        scratch_shapes=[
            tok, tok, V((256, 512), F32), V((56, 512), F32), V((56, 512), F32), V((512, 256), F32),
            tok, tok, nbr, nbr,
            V((8, 384, 512), BF), V((8, 384, 512), BF), V((8, 192, 896), BF),
            V((64, 16, 896), BF), V((16, 2, 16, 896), BF), V((16, 2, 16, 896), BF),
            V((8, 128), jnp.int32), V((16, 8, 128), jnp.int32), pltpu.SMEM((16, 8, 128), jnp.int32),
            V((8, 512, 512), BF), V((512, 4096), BF), V((896, 512), BF), V((896, 512), BF),
            tok, tok, nbr, nbr, wide, wide, V((896, 256), F32), V((896, 256), F32),
        ]
        + big + first + second
        + [V((4, 384, 512), BF), V((4, 384, 512), BF), V((4, 192, 896), BF)]
        + rings
        + [
            V((16, 2, 16, 896), BF),
            DMA((9,)), DMA((3, 8)), DMA((3, 8)), DMA((16,)), DMA((16,)), DMA((16,)), DMA((16,)),
            DMA((3,)), DMA((3,)), DMA((11, 6)), DMA((11, 6)), DMA((16,)), DMA((16,)), DMA((6,)),
        ],
        compiler_params=pltpu.CompilerParams(
            collective_id=1, has_side_effects=True, vmem_limit_bytes=64 * 2**20 - 2**17
        ),
    )(nbr_shard, nbr_row, hidden_in, cotangent, encodings, wq, wo, wk, wv)


def finish_kernel(want_s, ret, *refs):
    kept, out_ref, given = refs[:6], refs[6], refs[7:13]
    retv, held, encv, get, put = refs[13], refs[14:20], refs[20], refs[21], refs[22]
    arrive = pltpu.make_async_copy(ret, retv, get.at[6])
    arrive.start()
    ins = [pltpu.make_async_copy(a, b, get.at[n]) for n, (a, b) in enumerate(zip(kept, held))]
    outs = [pltpu.make_async_copy(a, b, put.at[n]) for n, (a, b) in enumerate(zip(held, given))]
    for one in ins:
        one.start()
    encv[...] = jnp.zeros_like(encv)
    arrive.wait()

    @pl.loop(0, 32, unroll=4)
    def _(s):
        row = want_s[s]
        encv[row] += retv[s // 2, s % 2].astype(F32)

    parts = [
        pltpu.make_async_copy(encv.at[pl.ds(n * 16, 16)], out_ref.at[pl.ds(n * 16, 16)], put.at[6 + n])
        for n in range(4)
    ]
    for one in parts:
        one.start()
    for one, two in zip(ins, outs):
        one.wait()
        two.start()
    for one in outs + parts:
        one.wait()


def finish_call(want, ret, kept):
    S = jax.ShapeDtypeStruct
    return pl.pallas_call(
        finish_kernel,
        name="finish",
        out_shape=(S((64, 16, 896), F32),) + tuple(S(a.shape, a.dtype) for a in kept),
        in_specs=[SM] + [ANY] * 7,
        out_specs=(ANY,) * 7,
        scratch_shapes=[pltpu.VMEM((16, 2, 16, 896), BF)]
        + [pltpu.VMEM(a.shape, a.dtype) for a in kept]
        + [pltpu.VMEM((64, 16, 896), F32), DMA((7,)), DMA((10,))],
        compiler_params=pltpu.CompilerParams(vmem_limit_bytes=64 * 2**20 - 2**17),
    )(want, ret, *kept)


def shards(hidden_in, encodings, nbr_shard, nbr_row, w_query, w_key, w_value, w_output, cotangent):
    wq = w_query.reshape(8, 512, 512)
    owners, rows = nbr_shard.T, nbr_row.T
    want, out, hid, ret, sq, sk, sv, so = layer_call(
        owners, rows, hidden_in, cotangent, encodings, wq, w_output, w_key, w_value
    )
    enc, out, hid, sq, sk, sv, so = finish_call(want, ret, (out, hid, sq, sk, sv, so))
    return (out, hid, enc, sq, sk, sv, so)


def solution(mesh):
    return jax.shard_map(
        shards,
        mesh=mesh,
        in_specs=(
            P("dp", "tensor"),
            P("dp", "tensor", None),
            P("dp", None),
            P("dp", None),
            P(None, "tensor"),
            P(None, "tensor"),
            P(None, "tensor"),
            P("tensor", None),
            P("dp", "tensor"),
        ),
        out_specs=(
            P("dp", "tensor"),
            P("dp", "tensor"),
            P("dp", "tensor", None),
            P("dp", "tensor"),
            P("dp", "tensor"),
            P("dp", "tensor"),
            P("tensor", "dp"),
        ),
        check_vma=False,
    )
```
